32 devices in a mesh: group: 2 (over y), expert: 8 (over z, core), dp: 2 (over x).
Axes of the slice: x: 2, y: 2, z: 4, core: 2. Of those that a mesh axis runs over, the one named last changes fastest.
Arguments:
- tokens: bfloat16 [2048, 7168], P(('group', 'expert'), 'dp'), parts along dimension 0, may hold values from -6 to 6
- expert_ids: int32 [2048, 8], P(('group', 'expert')), parts along dimension 0, may hold values from 0 to 15, all different within a row; in each aligned block of 128 rows (0 to 127, 128 to 255, ...) at most 96 rows name the same one
- route_weights: float32 [2048, 8], P(('group', 'expert')), parts along dimension 0, may hold values from 0.05 to 0.6
- w_gate: bfloat16 [16, 7168, 1024], P('expert', 'dp'), may hold values from -0.0625 to 0.0625
- w_up: bfloat16 [16, 7168, 1024], P('expert', 'dp'), may hold values from -0.0625 to 0.0625
- w_down: bfloat16 [16, 1024, 7168], P('expert', None, 'dp'), may hold values from -0.1875 to 0.1875
Outputs:
- combined: bfloat16 [2048, 7168], P(('group', 'expert'), 'dp'), parts along dimension 0
The draws below stay inside these ranges and needn't reach their ends.
There are 2 independent parts, one for each index of `group`. The reference program is written for one: setup_inputs(seed, part) draws one part's arguments, and reference() takes and returns one part's arrays. A program takes and returns all parts, laid end to end along the dimension named above; an argument that names none is the same for every part. Nothing has to cross between parts.
Inputs may be any that keep to these rules, and one draw needn't show every extreme that they name: `expert_ids`: each row names 8 different experts. In each aligned block of 128 rows (the tokens of one index of expert) no expert is named by more than 96 rows, a bound that some block reaches in some or all blocks.
All inputs are finite; a program needn't handle non-finite values.
Results may differ from the reference program's by a relative error of at most 0.015.
Values may be sent and summed in bfloat16 or wider, within the bound.
No kernel may reach another device: no remote copies, remote signals or barrier semaphores. Data moves between devices by JAX's collectives and lax.ppermute only.
A program may use at most 192 MiB of HBM per device.

```python
import math
import jax
import jax.numpy as jnp
import numpy as np
from jax import lax

D = 7168
TOPK = 8
FF = 1024
EXP_DEV = 2
COPIES = 2
TOK_COL = 128
EXPERTS = 16
TOKENS = 1024
CAP = 64
HOT = 96
N_EXPERT = 8
N_DP = 2


def level_of(key, dims, pieces, low, top_value):
    level = 1.0
    for dim, parts in pieces:
        draws = jax.random.uniform(jax.random.fold_in(jax.random.fold_in(key, 6), dim), (parts,), jnp.float32, low / len(pieces), top_value / len(pieces))
        level = level * jnp.repeat(jnp.exp(draws), dims[dim] // parts).reshape((-1,) + (1,) * (len(dims) - 1 - dim))
    return level


def deal_out(own_key, own, number, rows, count, top, reach, slope):
    ranking = jax.random.permutation(own_key, count)
    heavy_load, ordinary = portions_of(count, rows * top, reach, slope, True), portions_of(count, rows * top, reach, slope, False)
    places = jnp.arange(count)

    def named(lengths, offset_by):
        used = int((lengths > 0).sum())
        fixed = max(1, used // 4)
        shifted = fixed + (places - fixed + offset_by * (used - fixed)) % max(1, count - fixed)
        return jnp.zeros((count,), jnp.int32).at[ranking[jnp.where(places < fixed, places, shifted)]].set(jnp.asarray(lengths, jnp.int32))

    lengths = jnp.where(number % 4 == 0, named(heavy_load, number // 4), named(ordinary, number - number // 4 - 1))
    mixed = jax.random.permutation(jax.random.fold_in(own, 3), count)
    giver, sink = mixed[0:count // 2 * 2:2], mixed[1:count // 2 * 2:2]
    room = jnp.minimum(lengths[giver] - 1, reach - lengths[sink]) // 2
    room = jnp.where((giver == ranking[0]) | (sink == ranking[0]) | (lengths[sink] == 0), 0, jnp.maximum(room, 0))
    shifted = jax.random.randint(jax.random.fold_in(own, 4), (count // 2,), 0, 1 << 20) % (room + 1)
    lengths = lengths.at[giver].add(-shifted).at[sink].add(shifted)
    items = jnp.searchsorted(jnp.cumsum(lengths), jnp.arange(rows * top), side="right").astype(jnp.int32)
    listing = items.reshape(top, rows).T
    listing = listing[jax.random.permutation(jax.random.fold_in(own, 1), rows)]
    offset_by = jax.random.randint(jax.random.fold_in(own, 2), (rows, 1), 0, top)
    return jnp.take_along_axis(listing, (jnp.arange(top)[None, :] + offset_by) % top, axis=1)


def portions_of(number_of, total, most, slope, full):
    loads = [(1 << 20) // math.isqrt(grade ** slope) + 1 for grade in range(1, number_of + 1)]
    largest = most if full else min(most, max(-(-total // number_of), total * loads[0] // sum(loads)))
    least = 1 if total - largest >= number_of - 1 else 0
    given, surplus = [largest] + [least] * (number_of - 1), total - largest - least * (number_of - 1)
    while surplus > 0:
        free = [i for i in range(1, number_of) if given[i] < largest] or [i for i in range(1, number_of) if given[i] < most]
        whole, left = sum([loads[i] for i in free]), surplus
        for i in free:
            extra = min(most - given[i], max(1, left * loads[i] // whole), surplus)
            given[i] = given[i] + extra
            surplus = surplus - extra
    return np.array(given)


def normal_values(own_key, shape, scale, bound, cuts=(), kind=jnp.bfloat16):
    array = scale * jax.random.normal(own_key, shape, jnp.float32)
    if cuts:
        array = array * level_of(own_key, shape, cuts, -0.22, 0.18)
    return jnp.clip(array, -bound, bound).astype(kind)


def setup_inputs(seed: int = 0, part: int = 0) -> dict:
    keys = jax.random.split(jax.random.key(seed), 7)
    part_splits = jax.random.split(jax.random.fold_in(keys[6], part), 7)
    tokens = normal_values(part_splits[0], (TOKENS, D), 1.0, 6.0, ((0, 8), (1, 2)))
    expert_ids_keys = jax.random.split(jax.random.fold_in(part_splits[1], 1), TOKENS // TOK_COL)
    expert_ids_turns = jax.random.permutation(jax.random.fold_in(part_splits[1], 3), TOKENS // TOK_COL)
    expert_ids = jax.vmap(lambda own, number: deal_out(jax.random.fold_in(part_splits[1], 2), own, number, TOK_COL, EXPERTS, TOPK, HOT, 2))(expert_ids_keys, expert_ids_turns).reshape((TOKENS, TOPK))
    route_weights = jnp.clip(0.05 + 0.55 * jax.random.uniform(part_splits[2], (TOKENS, TOPK), jnp.float32) ** level_of(part_splits[2], (TOKENS, TOPK), ((0, 8),), -0.2, 0.2), 0.05, 0.6)
    w_gate = normal_values(keys[3], (EXPERTS, D, FF), D ** -0.5, 0.0625, ((0, 8), (1, 2)))
    w_up = normal_values(keys[4], (EXPERTS, D, FF), D ** -0.5, 0.0625, ((0, 8), (1, 2)))
    w_down = normal_values(keys[5], (EXPERTS, FF, D), FF ** -0.5, 0.1875, ((0, 8), (2, 2)))
    return {"tokens": tokens, "expert_ids": expert_ids, "route_weights": route_weights, "w_gate": w_gate, "w_up": w_up, "w_down": w_down}


def choose_copies(totals, exp_dev, columns, copies):
    per_column = totals.reshape(columns, exp_dev)
    col_load = jnp.sum(per_column, axis=1).astype(jnp.int32)
    col_order = jnp.arange(columns, dtype=jnp.int32)
    _, heavy_cols = lax.top_k(col_load * columns + (columns - 1 - col_order), copies)
    _, light_cols = lax.top_k(col_order - col_load * columns, copies)
    heavy_cols = heavy_cols.astype(jnp.int32)
    light_cols = light_cols.astype(jnp.int32)
    local_order = jnp.arange(exp_dev, dtype=jnp.int32)
    heavy_rows = per_column[heavy_cols]
    _, best_local = lax.top_k(heavy_rows * exp_dev + (exp_dev - 1 - local_order)[None, :], 1)
    copied_ids = heavy_cols * exp_dev + best_local[:, 0].astype(jnp.int32)
    return copied_ids.astype(jnp.int32), heavy_cols, light_cols


def reference(tokens, expert_ids, route_weights, w_gate, w_up, w_down):
    block_ids = expert_ids.reshape(N_EXPERT, TOK_COL * TOPK)
    onehot = (block_ids[:, :, None] == jnp.arange(EXPERTS, dtype=jnp.int32)[None, None, :]).astype(jnp.int32)
    order_rank = jnp.sum((jnp.cumsum(onehot, axis=1) - 1) * onehot, axis=2).astype(jnp.int32)
    totals = jnp.sum(onehot, axis=(0, 1)).astype(jnp.int32)
    copied_ids, heavy_cols, light_cols = choose_copies(totals, EXP_DEV, N_EXPERT, COPIES)
    is_copied = jnp.any(block_ids[:, :, None] == copied_ids[None, None, :], axis=2)
    kept_mask = ((order_rank < CAP) | (is_copied & (order_rank < HOT))).reshape(TOKENS, TOPK)
    kept_weights = jnp.where(kept_mask, route_weights, jnp.zeros_like(route_weights))
    row_count = N_EXPERT * HOT
    feat_block = D // N_DP

    def one_expert(combined, expert):
        named_here = (expert_ids == expert) & kept_mask
        hit_count = jnp.sum(named_here.astype(jnp.int32), axis=1).astype(jnp.int32)
        mixing = jnp.sum(jnp.where(named_here, kept_weights, jnp.zeros_like(kept_weights)), axis=1)
        chosen = jnp.argsort(1 - hit_count, stable=True)[:row_count].astype(jnp.int32)
        token_rows = tokens[chosen].astype(jnp.float32).reshape(row_count, N_DP, feat_block)
        gate_w = w_gate[expert].astype(jnp.float32).reshape(N_DP, feat_block, FF)
        up_w = w_up[expert].astype(jnp.float32).reshape(N_DP, feat_block, FF)
        gate_part = jnp.einsum("rpd,pdf->prf", token_rows, gate_w).astype(jnp.bfloat16)
        up_projection_piece = jnp.einsum("rpd,pdf->prf", token_rows, up_w).astype(jnp.bfloat16)
        gate_part, up_projection_piece = lax.optimization_barrier((gate_part, up_projection_piece))
        gate_sum = jnp.sum(gate_part.astype(jnp.float32), axis=0)
        up_sum = jnp.sum(up_projection_piece.astype(jnp.float32), axis=0)
        hidden = (jax.nn.silu(gate_sum) * up_sum).astype(jnp.bfloat16)
        expert_out = jnp.dot(hidden, w_down[expert], preferred_element_type=jnp.float32).astype(jnp.bfloat16)
        combined = combined.at[chosen].add(mixing[chosen][:, None] * expert_out.astype(jnp.float32))
        return combined, None

    combined, _ = lax.scan(one_expert, jnp.zeros((TOKENS, D), jnp.float32), jnp.arange(EXPERTS, dtype=jnp.int32))
    return combined.astype(jnp.bfloat16)
```

```python
import functools

import jax
import jax.numpy as jnp
from jax import lax
from jax.experimental import pallas as pl
from jax.experimental.pallas import tpu as pltpu
from jax.sharding import PartitionSpec as P

COPIES = 2
CORES = 2
LANES = 128
VMEM_LIMIT = 40 * 1024 * 1024


def capacities(token_column, selected_count, expert_table):
    slot_capacity = min(token_column * selected_count * 3 // (2 * expert_table), token_column // 2)
    popular_capacity = min(
        token_column, max(slot_capacity * 3 // 2, token_column * selected_count // expert_table)
    )
    return slot_capacity, popular_capacity


def round_up(value, unit):
    return -(-value // unit) * unit


def tile_of(size, most):
    return max(t for t in range(LANES, most + 1, LANES) if size % t == 0)


class Plan:
    def __init__(self, columns, exp_dev, token_column, selected_count, feat, hidden, parts):
        self.columns, self.exp_dev, self.tokens, self.topk = columns, exp_dev, token_column, selected_count
        self.feat, self.hidden, self.parts = feat, hidden, parts
        self.slot_cap, self.popular_cap = capacities(token_column, selected_count, columns * exp_dev)
        self.caps = [round_up(self.popular_cap, 16)] + [round_up(self.slot_cap, 16)] * (exp_dev - 1)
        self.starts = [CORES * sum(self.caps[:i]) for i in range(exp_dev)]
        self.rows = CORES * sum(self.caps)
        self.piece = hidden // parts

    def spans(self):
        for i, cap in enumerate(self.caps):
            for b in range(CORES):
                yield i, b, self.starts[i] + b * cap, cap


def local_of(i, first):
    return first if i == 0 else jnp.where(i - 1 < first, i - 1, i)


def route_kernel(pos_ref, info_ref, slot_ref, weight_ref, first_ref, *, plan):
    column = pos_ref[0]
    ids = info_ref[:, : plan.topk, :]
    weights = info_ref[:, plan.topk :, :]
    totals = [
        jnp.sum((ids == float(e)).astype(jnp.float32)) for e in range(plan.columns * plan.exp_dev)
    ]
    loads, best = [], []
    for c in range(plan.columns):
        own = totals[c * plan.exp_dev : (c + 1) * plan.exp_dev]
        load, top, where = own[0], own[0], jnp.int32(0)
        for i in range(1, plan.exp_dev):
            load = load + own[i]
            where = jnp.where(own[i] > top, i, where)
            top = jnp.maximum(own[i], top)
        loads.append(load)
        best.append(where)
    heavy_here = jnp.int32(0)
    for _ in range(COPIES):
        top, where = loads[0], jnp.int32(0)
        for c in range(1, plan.columns):
            where = jnp.where(loads[c] > top, c, where)
            top = jnp.maximum(loads[c], top)
        heavy_here = jnp.where(where == column, 1, heavy_here)
        loads = [jnp.where(where == c, -1.0, loads[c]) for c in range(plan.columns)]
    own_best = jnp.int32(0)
    for c in range(plan.columns):
        own_best = jnp.where(column == c, best[c], own_best)
    first = jnp.where(heavy_here == 1, own_best, 0)
    first_ref[0] = first
    earlier = (
        lax.broadcasted_iota(jnp.int32, (plan.tokens, plan.tokens), 0)
        < lax.broadcasted_iota(jnp.int32, (plan.tokens, plan.tokens), 1)
    ).astype(jnp.bfloat16)
    for i in range(plan.exp_dev):
        expert = (column * plan.exp_dev + local_of(i, first)).astype(jnp.float32)
        hit = ids == expert
        named = jnp.sum(hit.astype(jnp.float32), axis=1)
        weight_ref[i] = jnp.sum(jnp.where(hit, weights, 0.0), axis=1)
        rank = jnp.dot(named.astype(jnp.bfloat16), earlier, preferred_element_type=jnp.float32)
        cap = jnp.int32(plan.slot_cap)
        if i == 0:
            cap = jnp.where(heavy_here == 1, plan.popular_cap, cap)
        rank = rank.astype(jnp.int32)
        slot_ref[i] = jnp.where((named > 0.5) & (rank < cap), rank, -1)


def picks(slot_ref, i, block, cap):
    row = slot_ref[i, pl.ds(block, 1), :]
    return lax.broadcasted_iota(jnp.int32, (cap, row.shape[1]), 0) == row


def up_kernel(first_ref, pos_ref, slot_ref, mine_ref, other_ref, gate_ref, up_ref, out_ref, rows_ref, *, plan, at):
    @pl.when(pl.program_id(0) == 0)
    def _():
        step = tile_of(plan.feat, 512)
        for i, b, start, cap in plan.spans():
            select = picks(slot_ref, i, pos_ref[at + b], cap).astype(jnp.bfloat16)
            block_ref = (mine_ref, other_ref)[b]
            for k in range(0, plan.feat, step):
                rows_ref[start : start + cap, k : k + step] = jnp.dot(
                    select, block_ref[:, k : k + step], preferred_element_type=jnp.float32
                ).astype(jnp.bfloat16)

    first = first_ref[0]
    for i, cap in enumerate(plan.caps):
        local = local_of(i, first)
        span = slice(plan.starts[i], plan.starts[i] + CORES * cap)
        for half, weight_ref in enumerate((gate_ref, up_ref)):
            out_ref[half, span, :] = jnp.dot(
                rows_ref[span, :], weight_ref[local], preferred_element_type=jnp.float32
            ).astype(jnp.bfloat16)


def hidden_kernel(pos_ref, slot_ref, weight_ref, mine_ref, other_ref, out_ref, *, plan, at):
    for i, b, start, cap in plan.spans():
        block = pos_ref[at + b]
        chosen = picks(slot_ref, i, block, cap)
        scale = jnp.sum(jnp.where(chosen, weight_ref[i, pl.ds(block, 1), :], 0.0), axis=1, keepdims=True)
        span = slice(start, start + cap)
        gate = mine_ref[0, span, :].astype(jnp.float32) + other_ref[0, span, :].astype(jnp.float32)
        up = mine_ref[1, span, :].astype(jnp.float32) + other_ref[1, span, :].astype(jnp.float32)
        out_ref[span, :] = (gate / (1.0 + jnp.exp(-gate)) * up * scale).astype(jnp.bfloat16)


def down_kernel(first_ref, pos_ref, slot_ref, *refs, plan, at, part_at):
    pieces = refs[: plan.parts]
    down_ref, mine_ref, other_ref, dense_ref = refs[plan.parts :]

    @pl.when(pl.program_id(0) == 0)
    def _():
        first = first_ref[0]
        for i, b, start, cap in plan.spans():
            select = picks(slot_ref, i, pos_ref[at + b], cap).astype(jnp.bfloat16)
            for q, piece_ref in enumerate(pieces):
                offset = local_of(i, first) * plan.hidden + pos_ref[part_at + q] * plan.piece
                dense_ref[
                    b * plan.tokens : (b + 1) * plan.tokens,
                    pl.ds(pl.multiple_of(offset, LANES), plan.piece),
                ] = lax.dot_general(
                    select,
                    piece_ref[start : start + cap, :],
                    (((0,), (0,)), ((), ())),
                    preferred_element_type=jnp.float32,
                ).astype(jnp.bfloat16)

    weight = down_ref[...].reshape(plan.exp_dev * plan.hidden, down_ref.shape[2])
    total = jnp.dot(dense_ref[...], weight, preferred_element_type=jnp.float32)
    mine_ref[...] = total[: plan.tokens].astype(jnp.bfloat16)
    other_ref[...] = total[plan.tokens :].astype(jnp.bfloat16)


def whole(shape):
    return pl.BlockSpec(shape, lambda *_: (0,) * len(shape))


def call_route(plan, pos, info):
    lists = jax.ShapeDtypeStruct((plan.exp_dev, plan.columns, plan.tokens), jnp.int32)
    return pl.pallas_call(
        functools.partial(route_kernel, plan=plan),
        out_shape=(
            lists,
            jax.ShapeDtypeStruct(lists.shape, jnp.float32),
            jax.ShapeDtypeStruct((1,), jnp.int32),
        ),
        in_specs=[pl.BlockSpec(memory_space=pltpu.SMEM), pl.BlockSpec(memory_space=pltpu.VMEM)],
        out_specs=(
            pl.BlockSpec(memory_space=pltpu.VMEM),
            pl.BlockSpec(memory_space=pltpu.VMEM),
            pl.BlockSpec(memory_space=pltpu.SMEM),
        ),
        name="route",
    )(pos, info)


def call_up(plan, route, pos, mine, other, w_gate, w_up, at, part):
    slot, _, first = route
    units = plan.hidden if part is None else plan.piece
    tile = tile_of(plan.piece, 256)
    tiles = units // tile

    def weight_at(j, first_ref, pos_ref):
        return 0, 0, j if part is None else pos_ref[part] * tiles + j

    weight = pl.BlockSpec((plan.exp_dev, plan.feat, tile), weight_at)
    block = whole((plan.tokens, plan.feat))
    return pl.pallas_call(
        functools.partial(up_kernel, plan=plan, at=at),
        out_shape=jax.ShapeDtypeStruct((2, plan.rows, units), jnp.bfloat16),
        grid_spec=pltpu.PrefetchScalarGridSpec(
            num_scalar_prefetch=2,
            grid=(tiles,),
            in_specs=[whole(slot.shape), block, block, weight, weight],
            out_specs=pl.BlockSpec((2, plan.rows, tile), lambda j, *_: (0, 0, j)),
            scratch_shapes=[pltpu.VMEM((plan.rows, plan.feat), jnp.bfloat16)],
        ),
        compiler_params=pltpu.CompilerParams(vmem_limit_bytes=VMEM_LIMIT),
        cost_estimate=pl.CostEstimate(
            flops=4 * plan.rows * plan.feat * units,
            bytes_accessed=4 * plan.exp_dev * plan.feat * units,
            transcendentals=0,
        ),
        name="gate_up",
    )(first, pos, slot, mine, other, w_gate, w_up)


def call_hidden(plan, route, pos, mine, other, at):
    slot, weight, _ = route
    vmem = pl.BlockSpec(memory_space=pltpu.VMEM)
    return pl.pallas_call(
        functools.partial(hidden_kernel, plan=plan, at=at),
        out_shape=jax.ShapeDtypeStruct((plan.rows, plan.piece), jnp.bfloat16),
        in_specs=[pl.BlockSpec(memory_space=pltpu.SMEM)] + [vmem] * 4,
        out_specs=vmem,
        compiler_params=pltpu.CompilerParams(vmem_limit_bytes=VMEM_LIMIT),
        cost_estimate=pl.CostEstimate(
            flops=8 * plan.rows * plan.piece,
            bytes_accessed=10 * plan.rows * plan.piece,
            transcendentals=plan.rows * plan.piece,
        ),
        name="hidden",
    )(pos, slot, weight, mine, other)


def call_down(plan, route, pos, pieces, w_down, at, part_at):
    slot, _, first = route
    tile = tile_of(plan.feat, 512)
    out = jax.ShapeDtypeStruct((plan.tokens, plan.feat), jnp.bfloat16)
    out_block = pl.BlockSpec((plan.tokens, tile), lambda j, *_: (0, j))
    return pl.pallas_call(
        functools.partial(down_kernel, plan=plan, at=at, part_at=part_at),
        out_shape=(out, out),
        grid_spec=pltpu.PrefetchScalarGridSpec(
            num_scalar_prefetch=2,
            grid=(plan.feat // tile,),
            in_specs=[whole(slot.shape)]
            + [whole((plan.rows, plan.piece))] * plan.parts
            + [pl.BlockSpec((plan.exp_dev, plan.hidden, tile), lambda j, *_: (0, 0, j))],
            out_specs=(out_block, out_block),
            scratch_shapes=[
                pltpu.VMEM((CORES * plan.tokens, plan.exp_dev * plan.hidden), jnp.bfloat16)
            ],
        ),
        compiler_params=pltpu.CompilerParams(vmem_limit_bytes=VMEM_LIMIT),
        cost_estimate=pl.CostEstimate(
            flops=2 * CORES * plan.tokens * plan.exp_dev * plan.hidden * plan.feat,
            bytes_accessed=2 * plan.exp_dev * plan.hidden * plan.feat,
            transcendentals=0,
        ),
        name="down",
    )(first, pos, slot, *pieces, w_down)


def per_device(tokens, expert_ids, route_weights, w_gate, w_up, w_down):
    columns, parts = lax.axis_size("expert"), lax.axis_size("dp")
    chips = columns // CORES
    column, part = lax.axis_index("expert"), lax.axis_index("dp")
    chip, core = column // CORES, column % CORES
    plan = Plan(
        columns, w_gate.shape[0], *expert_ids.shape, tokens.shape[1], w_gate.shape[2], parts
    )

    def hop(x, pairs):
        return lax.ppermute(
            x, "expert", [(a * CORES + c, b * CORES + c) for a, b in pairs for c in range(CORES)]
        )

    def swap_cores(x):
        return lax.ppermute(x, "expert", [(i, i ^ 1) for i in range(columns)])

    info = jnp.concatenate([expert_ids.T.astype(jnp.float32), route_weights.T], axis=0)
    info = lax.all_gather(info, "expert", axis=0)

    arrived, source, back = [tokens], [chip], [None]
    if chips == 4:
        near = [(0, 1), (1, 0), (2, 3), (3, 2)]
        middle = [(1, 2), (2, 1)]
        outward = [(1, 0), (2, 3)]
        inner = (chip == 1) | (chip == 2)
        a1 = hop(tokens, near)
        a2 = hop(tokens, middle)
        b1 = hop(a1, middle)
        b2 = hop(a2, outward)
        c1 = hop(b1, outward)
        arrived += [a1, jnp.where(inner, a2, b2), jnp.where(inner, b1, c1)]
        source += [chip ^ 1, jnp.where(chip < 2, 2, 1), jnp.where(chip < 2, 3, 0)]
        back += [
            [near],
            [middle, [(0, 2), (3, 1)]],
            [[(0, 3), (3, 0)], [(1, 3), (2, 0)]],
        ]
    else:
        for s in range(1, chips):
            arrived.append(hop(tokens, [(z, (z + s) % chips) for z in range(chips)]))
            source.append((chip - s) % chips)
            back.append([[(z, (z - s) % chips) for z in range(chips)]])

    values = [column]
    for s in source:
        values += [s * CORES + core, s * CORES + 1 - core]
    part_at = len(values)
    values += [part, 1 - part] if parts == 2 else list(range(parts))
    pos = jnp.stack([jnp.asarray(v, jnp.int32) for v in values])

    route = call_route(plan, pos, info)
    total = []
    for s in range(chips):
        at = 1 + CORES * s
        mine = arrived[s]
        other = swap_cores(mine)
        if parts == 2:
            flip = [(0, 1), (1, 0)]
            away = call_up(plan, route, pos, mine, other, w_gate, w_up, at, part_at + 1)
            away = lax.ppermute(away, "dp", flip)
            here = call_up(plan, route, pos, mine, other, w_gate, w_up, at, part_at)
            hidden = call_hidden(plan, route, pos, here, away, at)
            pieces = [hidden, lax.ppermute(hidden, "dp", flip)]
        else:
            both = call_up(plan, route, pos, mine, other, w_gate, w_up, at, None)
            both = lax.psum_scatter(both, "dp", scatter_dimension=2, tiled=True)
            hidden = call_hidden(plan, route, pos, both, jnp.zeros_like(both), at)
            hidden = lax.all_gather(hidden, "dp", axis=0)
            pieces = [hidden[q] for q in range(parts)]
        kept, sent = call_down(plan, route, pos, pieces, w_down, at, part_at)
        summed = kept.astype(jnp.float32) + swap_cores(sent).astype(jnp.float32)
        if s == 0:
            total.append(summed)
        else:
            total += [hop(summed.astype(jnp.bfloat16), pairs) for pairs in back[s]]
    return sum(t.astype(jnp.float32) for t in total).astype(jnp.bfloat16)


def solution(mesh):
    in_specs = (
        P(("group", "expert"), "dp"),
        P(("group", "expert"), None),
        P(("group", "expert"), None),
        P("expert", "dp", None),
        P("expert", "dp", None),
        P("expert", None, "dp"),
    )
    out_specs = P(("group", "expert"), "dp")
    return jax.shard_map(
        per_device, mesh=mesh, in_specs=in_specs, out_specs=out_specs, check_vma=False
    )
```

```python
import functools

import jax
import jax.numpy as jnp
from jax import lax
from jax.experimental import pallas as pl
from jax.experimental.pallas import tpu as pltpu
from jax.sharding import PartitionSpec as P

COPIES = 2
CORES = 2
LANES = 128
VMEM_LIMIT = 4 * 1024 * 1024
UP_LIMIT = 9 * 1024 * 1024
DOWN_LIMIT = 12 * 1024 * 1024
BUFFERS = 2


def capacities(token_column, selected_count, expert_table):
    slot_capacity = min(token_column * selected_count * 3 // (2 * expert_table), token_column // 2)
    popular_capacity = min(
        token_column, max(slot_capacity * 3 // 2, token_column * selected_count // expert_table)
    )
    return slot_capacity, popular_capacity


def round_up(value, unit):
    return -(-value // unit) * unit


def tile_of(size, most):
    return max(t for t in range(LANES, most + 1, LANES) if size % t == 0)


class Plan:
    def __init__(self, columns, exp_dev, token_column, selected_count, feat, hidden, parts):
        self.columns, self.exp_dev, self.tokens, self.topk = columns, exp_dev, token_column, selected_count
        self.feat, self.hidden, self.parts = feat, hidden, parts
        self.slot_cap, self.popular_cap = capacities(token_column, selected_count, columns * exp_dev)
        self.caps = [round_up(self.popular_cap, 16)] + [round_up(self.slot_cap, 16)] * (exp_dev - 1)
        self.starts = [CORES * sum(self.caps[:i]) for i in range(exp_dev)]
        self.rows = CORES * sum(self.caps)
        self.piece = hidden // parts

    def spans(self):
        for i, cap in enumerate(self.caps):
            for b in range(CORES):
                yield i, b, self.starts[i] + b * cap, cap


def local_of(i, first):
    return first if i == 0 else jnp.where(i - 1 < first, i - 1, i)


def route_kernel(pos_ref, *refs, plan):
    slot_ref, weight_ref, first_ref = refs[-3:]
    column = pos_ref[0]
    info = jnp.concatenate([ref[...] for ref in refs[:-3]], axis=0)
    ids = info[:, : plan.topk, :]
    weights = info[:, plan.topk :, :]
    totals = [
        jnp.sum((ids == float(e)).astype(jnp.float32)) for e in range(plan.columns * plan.exp_dev)
    ]
    loads, best = [], []
    for c in range(plan.columns):
        own = totals[c * plan.exp_dev : (c + 1) * plan.exp_dev]
        load, top, where = own[0], own[0], jnp.int32(0)
        for i in range(1, plan.exp_dev):
            load = load + own[i]
            where = jnp.where(own[i] > top, i, where)
            top = jnp.maximum(own[i], top)
        loads.append(load)
        best.append(where)
    heavy_here = jnp.int32(0)
    for _ in range(COPIES):
        top, where = loads[0], jnp.int32(0)
        for c in range(1, plan.columns):
            where = jnp.where(loads[c] > top, c, where)
            top = jnp.maximum(loads[c], top)
        heavy_here = jnp.where(where == column, 1, heavy_here)
        loads = [jnp.where(where == c, -1.0, loads[c]) for c in range(plan.columns)]
    own_best = jnp.int32(0)
    for c in range(plan.columns):
        own_best = jnp.where(column == c, best[c], own_best)
    first = jnp.where(heavy_here == 1, own_best, 0)
    first_ref[0] = first
    earlier = (
        lax.broadcasted_iota(jnp.int32, (plan.tokens, plan.tokens), 0)
        < lax.broadcasted_iota(jnp.int32, (plan.tokens, plan.tokens), 1)
    ).astype(jnp.bfloat16)
    for i in range(plan.exp_dev):
        expert = (column * plan.exp_dev + local_of(i, first)).astype(jnp.float32)
        hit = ids == expert
        named = jnp.sum(hit.astype(jnp.float32), axis=1)
        weight_ref[i] = jnp.sum(jnp.where(hit, weights, 0.0), axis=1)
        rank = jnp.dot(named.astype(jnp.bfloat16), earlier, preferred_element_type=jnp.float32)
        cap = jnp.int32(plan.slot_cap)
        if i == 0:
            cap = jnp.where(heavy_here == 1, plan.popular_cap, cap)
        rank = rank.astype(jnp.int32)
        slot_ref[i] = jnp.where((named > 0.5) & (rank < cap), rank, -1)


def picks(slot_ref, i, block, cap):
    row = slot_ref[i, pl.ds(block, 1), :]
    return lax.broadcasted_iota(jnp.int32, (cap, row.shape[1]), 0) == row


def up_kernel(first_ref, pos_ref, slot_ref, mine_ref, other_ref, gate_ref, up_ref, out_ref, rows_ref, *, plan, at, part):
    step = tile_of(plan.feat, 512)
    for i, b, start, cap in plan.spans():
        select = picks(slot_ref, i, pos_ref[at + b], cap).astype(jnp.bfloat16)
        block_ref = (mine_ref, other_ref)[b]
        for k in range(0, plan.feat, step):
            rows_ref[start : start + cap, k : k + step] = jnp.dot(
                select, block_ref[:, k : k + step], preferred_element_type=jnp.float32
            ).astype(jnp.bfloat16)

    first = first_ref[0]
    for q in range(out_ref.shape[2] // plan.piece):
        units = pl.ds(pl.multiple_of((q if part is None else pos_ref[part]) * plan.piece, LANES), plan.piece)
        for i, cap in enumerate(plan.caps):
            local = local_of(i, first)
            span = slice(plan.starts[i], plan.starts[i] + CORES * cap)
            for half, weight_ref in enumerate((gate_ref, up_ref)):
                out_ref[half, span, q * plan.piece : (q + 1) * plan.piece] = jnp.dot(
                    rows_ref[span, :], weight_ref[local, :, units], preferred_element_type=jnp.float32
                ).astype(jnp.bfloat16)


def hidden_kernel(pos_ref, slot_ref, weight_ref, mine_ref, other_ref, out_ref, *, plan, at):
    for i, b, start, cap in plan.spans():
        block = pos_ref[at + b]
        chosen = picks(slot_ref, i, block, cap)
        scale = jnp.sum(jnp.where(chosen, weight_ref[i, pl.ds(block, 1), :], 0.0), axis=1, keepdims=True)
        span = slice(start, start + cap)
        gate = mine_ref[0, span, :].astype(jnp.float32) + other_ref[0, span, :].astype(jnp.float32)
        up = mine_ref[1, span, :].astype(jnp.float32) + other_ref[1, span, :].astype(jnp.float32)
        out_ref[span, :] = (gate / (1.0 + jnp.exp(-gate)) * up * scale).astype(jnp.bfloat16)


def down_kernel(first_ref, pos_ref, slot_ref, *refs, plan, at, part_at):
    pieces = refs[: plan.parts]
    down_ref, mine_ref, other_ref, dense_ref, tiles_ref, done = refs[plan.parts :]
    buffers, tile = tiles_ref.shape[0], tiles_ref.shape[3]
    copies = [
        pltpu.make_async_copy(
            down_ref.at[:, :, k * tile : (k + 1) * tile], tiles_ref.at[k % buffers], done.at[k]
        )
        for k in range(plan.feat // tile)
    ]
    for copy in copies[:buffers]:
        copy.start()
    first = first_ref[0]
    for i, b, start, cap in plan.spans():
        select = picks(slot_ref, i, pos_ref[at + b], cap).astype(jnp.bfloat16)
        for q, piece_ref in enumerate(pieces):
            offset = local_of(i, first) * plan.hidden + pos_ref[part_at + q] * plan.piece
            dense_ref[
                b * plan.tokens : (b + 1) * plan.tokens,
                pl.ds(pl.multiple_of(offset, LANES), plan.piece),
            ] = lax.dot_general(
                select,
                piece_ref[start : start + cap, :],
                (((0,), (0,)), ((), ())),
                preferred_element_type=jnp.float32,
            ).astype(jnp.bfloat16)

    for k, copy in enumerate(copies):
        copy.wait()
        weight = tiles_ref[k % buffers].reshape(plan.exp_dev * plan.hidden, tile)
        total = jnp.dot(dense_ref[...], weight, preferred_element_type=jnp.float32)
        span = slice(k * tile, (k + 1) * tile)
        mine_ref[:, span] = total[: plan.tokens].astype(jnp.bfloat16)
        other_ref[:, span] = total[plan.tokens :].astype(jnp.bfloat16)
        if k + buffers < len(copies):
            copies[k + buffers].start()


SMEM = pl.BlockSpec(memory_space=pltpu.SMEM)
VMEM = pl.BlockSpec(memory_space=pltpu.VMEM)
PARAMS = pltpu.CompilerParams(vmem_limit_bytes=VMEM_LIMIT)
COST = pl.CostEstimate(flops=1000, bytes_accessed=1000, transcendentals=0)


def after(x, *others):
    return lax.optimization_barrier((x, *others))[0]


class Order:
    def __init__(self, pos):
        self.pos = pos

    def follow(self, *results):
        self.pos = after(self.pos, *results)

    def run(self, call):
        result = call(self.pos)
        self.follow(*jax.tree.leaves(result))
        return result


def held(x):
    return pltpu.with_memory_space_constraint(x, pltpu.VMEM)


def call_route(plan, pos, infos):
    lists = jax.ShapeDtypeStruct((plan.exp_dev, plan.columns, plan.tokens), jnp.int32)
    return pl.pallas_call(
        functools.partial(route_kernel, plan=plan),
        out_shape=(
            lists,
            jax.ShapeDtypeStruct(lists.shape, jnp.float32),
            jax.ShapeDtypeStruct((1,), jnp.int32),
        ),
        in_specs=[SMEM] + [VMEM] * len(infos),
        out_specs=(VMEM, VMEM, SMEM),
        compiler_params=PARAMS,
        cost_estimate=COST,
        name="route",
    )(pos, *infos)


def call_up(plan, route, pos, mine, other, w_gate, w_up, at, part):
    slot, _, first = route
    return pl.pallas_call(
        functools.partial(up_kernel, plan=plan, at=at, part=part),
        out_shape=jax.ShapeDtypeStruct(
            (2, plan.rows, plan.hidden if part is None else plan.piece), jnp.bfloat16
        ),
        in_specs=[SMEM, SMEM] + [VMEM] * 5,
        out_specs=VMEM,
        scratch_shapes=[pltpu.VMEM((plan.rows, plan.feat), jnp.bfloat16)],
        compiler_params=pltpu.CompilerParams(vmem_limit_bytes=UP_LIMIT),
        cost_estimate=COST,
        name="gate_up",
    )(first, pos, slot, mine, other, held(w_gate), held(w_up))


def call_hidden(plan, route, pos, mine, other, at):
    slot, weight, _ = route
    return pl.pallas_call(
        functools.partial(hidden_kernel, plan=plan, at=at),
        out_shape=jax.ShapeDtypeStruct((plan.rows, plan.piece), jnp.bfloat16),
        in_specs=[SMEM] + [VMEM] * 4,
        out_specs=VMEM,
        compiler_params=PARAMS,
        cost_estimate=COST,
        name="hidden",
    )(pos, slot, weight, mine, other)


def call_down(plan, route, pos, pieces, w_down, at, part_at):
    slot, _, first = route
    tile = tile_of(plan.feat, 896)
    out = jax.ShapeDtypeStruct((plan.tokens, plan.feat), jnp.bfloat16)
    return pl.pallas_call(
        functools.partial(down_kernel, plan=plan, at=at, part_at=part_at),
        out_shape=(out, out),
        in_specs=[SMEM, SMEM] + [VMEM] * (1 + plan.parts) + [pl.BlockSpec(memory_space=pltpu.HBM)],
        out_specs=(VMEM, VMEM),
        scratch_shapes=[
            pltpu.VMEM((CORES * plan.tokens, plan.exp_dev * plan.hidden), jnp.bfloat16),
            pltpu.VMEM((BUFFERS, plan.exp_dev, plan.hidden, tile), jnp.bfloat16),
            pltpu.SemaphoreType.DMA((plan.feat // tile,)),
        ],
        compiler_params=pltpu.CompilerParams(vmem_limit_bytes=DOWN_LIMIT),
        cost_estimate=COST,
        name="down",
    )(first, pos, slot, *pieces, pltpu.with_memory_space_constraint(w_down, pltpu.HBM))


def per_device(tokens, expert_ids, route_weights, w_gate, w_up, w_down):
    columns, parts = lax.axis_size("expert"), lax.axis_size("dp")
    chips = columns // CORES
    column, part = lax.axis_index("expert"), lax.axis_index("dp")
    chip, core = column // CORES, column % CORES
    plan = Plan(
        columns, w_gate.shape[0], *expert_ids.shape, tokens.shape[1], w_gate.shape[2], parts
    )

    def hop(x, pairs):
        return lax.ppermute(
            x, "expert", [(a * CORES + c, b * CORES + c) for a, b in pairs for c in range(CORES)]
        )

    def swap_cores(x):
        return lax.ppermute(x, "expert", [(i, i ^ 1) for i in range(columns)])

    values, at = [column], []

    def list_blocks(source):
        away = (chip - source) % chips
        at.append(len(values))
        values.extend([away, chips + away])

    if chips == 4:
        sources = [chip, chip ^ 1, chip ^ 2, 3 - chip]
    else:
        sources = [(chip - s) % chips for s in range(chips)]
    for source in sources:
        list_blocks(source)
    part_at = len(values)
    values += [part, 1 - part] if parts == 2 else list(range(parts))
    pos = jnp.stack([jnp.asarray(v, jnp.int32) for v in values])

    def shift(s):
        return [(z, (z + s) % chips) for z in range(chips)]

    info = jnp.concatenate([expert_ids.T.astype(jnp.float32), route_weights.T], axis=0)
    info = [info] + [hop(info, shift(s)) for s in range(1, chips)]
    sent = after(tokens, *info[1:])
    info = jnp.stack(info)
    infos = [info, swap_cores(info)]

    inner = (chip == 1) | (chip == 2)
    near, middle, outward = [(0, 1), (1, 0), (2, 3), (3, 2)], [(1, 2), (2, 1)], [(1, 0), (2, 3)]
    if chips == 4:
        first, third = hop(sent, near), hop(sent, middle)
    else:
        first, *rest = [hop(sent, shift(s)) for s in range(1, chips)] or [None]

    flip = [(0, 1), (1, 0)]
    order = Order(pos)
    route = order.run(lambda pos: call_route(plan, pos, infos))

    def up(s, mine, other, which):
        piece = None if parts != 2 else part_at + which
        return order.run(lambda pos: call_up(plan, route, pos, mine, other, w_gate, w_up, at[s], piece))

    here, away, hidden, total = {}, {}, {}, {}

    def start(s, mine, other):
        if parts == 2:
            away[s] = lax.ppermute(up(s, mine, other, 1), "dp", flip)
        else:
            both = lax.psum_scatter(up(s, mine, other, 0), "dp", scatter_dimension=2, tiled=True)
            here[s], away[s] = both, jnp.zeros_like(both)

    def keep(s, mine, other):
        if parts == 2:
            here[s] = up(s, mine, other, 0)

    def join(s):
        own = order.run(lambda pos: call_hidden(plan, route, pos, here[s], away[s], at[s]))
        if parts == 2:
            hidden[s] = [own, lax.ppermute(own, "dp", flip)]
        else:
            own = lax.all_gather(own, "dp", axis=0)
            hidden[s] = [own[q] for q in range(parts)]

    def down(s):
        kept, shared = order.run(
            lambda pos: call_down(plan, route, pos, hidden[s], w_down, at[s], part_at)
        )
        total[s] = kept, swap_cores(shared)

    def send(s):
        summed = total[s][0].astype(jnp.float32) + total[s][1].astype(jnp.float32)
        relay = chips == 4 and s == 3
        if relay:
            (passed,) = total[2]
            summed += jnp.where(inner, passed, jnp.zeros_like(passed)).astype(jnp.float32)
            total[2] = (jnp.where(inner, jnp.zeros_like(passed), passed),)
        summed = summed.astype(jnp.bfloat16)
        order.follow(summed)
        if chips == 4:
            pairs = [near, [(0, 1), (1, 3), (2, 0), (3, 2)], [(0, 3), (1, 2), (2, 1), (3, 0)]][s - 1]
        else:
            pairs = shift(-s)
        total[s] = (hop(summed, pairs),)

    blocks = {0: [tokens, swap_cores(sent)]}

    def take(s, block):
        blocks[s] = [block, swap_cores(block)]

    def begin(s):
        start(s, *blocks[s])

    def go_on(s):
        keep(s, *blocks[s])

    begin(0)
    go_on(0)
    if chips == 4:
        first, third = after(first, order.pos), after(third, order.pos)
        take(1, first)
        relayed, other = hop(first, middle), hop(third, outward)
        join(0)
        begin(1)
        down(0)
        go_on(1)
        relayed = after(relayed, order.pos)
        take(2, jnp.where(inner, relayed, other))
        last = hop(relayed, outward)
        join(1)
        begin(2)
        down(1)
        go_on(2)
        join(2)
        send(1)
        take(3, jnp.where(inner, third, after(last, order.pos)))
        begin(3)
        down(2)
        go_on(3)
        join(3)
        order.follow(*total[1])
        send(2)
        down(3)
        send(3)
    else:
        join(0)
        down(0)
        for s in range(1, chips):
            take(s, [first, *rest][s - 1])
            begin(s)
            go_on(s)
            join(s)
            down(s)
            send(s)
    return sum(t.astype(jnp.float32) for s in range(chips) for t in total[s]).astype(jnp.bfloat16)


def solution(mesh):
    in_specs = (
        P(("group", "expert"), "dp"),
        P(("group", "expert"), None),
        P(("group", "expert"), None),
        P("expert", "dp", None),
        P("expert", "dp", None),
        P("expert", None, "dp"),
    )
    out_specs = P(("group", "expert"), "dp")
    return jax.shard_map(
        per_device, mesh=mesh, in_specs=in_specs, out_specs=out_specs, check_vma=False
    )
```

```python
import functools

import jax
import jax.numpy as jnp
from jax import lax
from jax.experimental import pallas as pl
from jax.experimental.pallas import tpu as pltpu
from jax.sharding import PartitionSpec as P

COPIES = 2
CORES = 2
LANES = 128
VMEM_LIMIT = 4 * 1024 * 1024
UP_LIMIT = 46 * 1024 * 1024
DOWN_LIMIT = 24 * 1024 * 1024
BUFFERS = 4


def capacities(token_column, selected_count, expert_table):
    slot_capacity = min(token_column * selected_count * 3 // (2 * expert_table), token_column // 2)
    popular_capacity = min(
        token_column, max(slot_capacity * 3 // 2, token_column * selected_count // expert_table)
    )
    return slot_capacity, popular_capacity


def round_up(value, unit):
    return -(-value // unit) * unit


def tile_of(size, most):
    return max(t for t in range(LANES, most + 1, LANES) if size % t == 0)


class Plan:
    def __init__(self, columns, exp_dev, token_column, selected_count, feat, hidden, parts):
        self.columns, self.exp_dev, self.tokens, self.topk = columns, exp_dev, token_column, selected_count
        self.feat, self.hidden, self.parts = feat, hidden, parts
        self.slot_cap, self.popular_cap = capacities(token_column, selected_count, columns * exp_dev)
        self.caps = [round_up(self.popular_cap, 16)] + [round_up(self.slot_cap, 16)] * (exp_dev - 1)
        self.starts = [CORES * sum(self.caps[:i]) for i in range(exp_dev)]
        self.rows = CORES * sum(self.caps)
        self.piece = hidden // parts

    def spans(self):
        for i, cap in enumerate(self.caps):
            for b in range(CORES):
                yield i, b, self.starts[i] + b * cap, cap


def local_of(i, first):
    return first if i == 0 else jnp.where(i - 1 < first, i - 1, i)


def route_kernel(pos_ref, *refs, plan):
    slot_ref, weight_ref, first_ref = refs[-3:]
    column = pos_ref[0]
    info = jnp.concatenate([ref[...] for ref in refs[:-3]], axis=0)
    ids = info[:, : plan.topk, :]
    weights = info[:, plan.topk :, :]
    totals = [
        jnp.sum((ids == float(e)).astype(jnp.float32)) for e in range(plan.columns * plan.exp_dev)
    ]
    loads, best = [], []
    for c in range(plan.columns):
        own = totals[c * plan.exp_dev : (c + 1) * plan.exp_dev]
        load, top, where = own[0], own[0], jnp.int32(0)
        for i in range(1, plan.exp_dev):
            load = load + own[i]
            where = jnp.where(own[i] > top, i, where)
            top = jnp.maximum(own[i], top)
        loads.append(load)
        best.append(where)
    heavy_here = jnp.int32(0)
    for _ in range(COPIES):
        top, where = loads[0], jnp.int32(0)
        for c in range(1, plan.columns):
            where = jnp.where(loads[c] > top, c, where)
            top = jnp.maximum(loads[c], top)
        heavy_here = jnp.where(where == column, 1, heavy_here)
        loads = [jnp.where(where == c, -1.0, loads[c]) for c in range(plan.columns)]
    own_best = jnp.int32(0)
    for c in range(plan.columns):
        own_best = jnp.where(column == c, best[c], own_best)
    first = jnp.where(heavy_here == 1, own_best, 0)
    first_ref[0] = first
    earlier = (
        lax.broadcasted_iota(jnp.int32, (plan.tokens, plan.tokens), 0)
        < lax.broadcasted_iota(jnp.int32, (plan.tokens, plan.tokens), 1)
    ).astype(jnp.bfloat16)
    for i in range(plan.exp_dev):
        expert = (column * plan.exp_dev + local_of(i, first)).astype(jnp.float32)
        hit = ids == expert
        named = jnp.sum(hit.astype(jnp.float32), axis=1)
        weight_ref[i] = jnp.sum(jnp.where(hit, weights, 0.0), axis=1)
        rank = jnp.dot(named.astype(jnp.bfloat16), earlier, preferred_element_type=jnp.float32)
        cap = jnp.int32(plan.slot_cap)
        if i == 0:
            cap = jnp.where(heavy_here == 1, plan.popular_cap, cap)
        rank = rank.astype(jnp.int32)
        slot_ref[i] = jnp.where((named > 0.5) & (rank < cap), rank, -1)


def picks(slot_ref, i, block, cap):
    row = slot_ref[i, pl.ds(block, 1), :]
    return lax.broadcasted_iota(jnp.int32, (cap, row.shape[1]), 0) == row


def up_kernel(
    first_ref, pos_ref, slot_ref, mine_ref, other_ref, gate_ref, up_ref, *refs, plan, at, part_at
):
    outs, (rows_ref, sums_ref, held_ref, done) = refs[: plan.parts], refs[plan.parts :]
    pieces = held_ref.shape[0] // (2 * plan.exp_dev)
    depth = held_ref.shape[1]
    first = first_ref[0]
    units = [(k, i, half) for k in range(pieces) for i in range(plan.exp_dev) for half in range(2)]
    copies = [
        pltpu.make_async_copy(
            (gate_ref, up_ref)[half].at[local_of(i, first), k * depth : (k + 1) * depth, :],
            held_ref.at[n],
            done.at[n],
        )
        for n, (k, i, half) in enumerate(units)
    ]
    for copy in copies:
        copy.start()
    step = tile_of(plan.feat, 512)
    for i, b, start, cap in plan.spans():
        select = picks(slot_ref, i, pos_ref[at + b], cap).astype(jnp.bfloat16)
        block_ref = (mine_ref, other_ref)[b]
        for k in range(0, plan.feat, step):
            rows_ref[start : start + cap, k : k + step] = jnp.dot(
                select, block_ref[:, k : k + step], preferred_element_type=jnp.float32
            ).astype(jnp.bfloat16)

    for n, (k, i, half) in enumerate(units):
        span = slice(plan.starts[i], plan.starts[i] + CORES * plan.caps[i])
        copies[n].wait()
        if k < pieces - 1:
            sums = jnp.dot(
                rows_ref[span, k * depth : (k + 1) * depth],
                held_ref[n],
                preferred_element_type=jnp.float32,
            )
            sums_ref[half, span, :] = sums if k == 0 else sums_ref[half, span, :] + sums
            continue
        for q, out_ref in enumerate(outs):
            columns = pl.ds(pl.multiple_of(pos_ref[part_at + q] * plan.piece, LANES), plan.piece)
            sums = jnp.dot(
                rows_ref[span, k * depth : (k + 1) * depth],
                held_ref[n, :, columns],
                preferred_element_type=jnp.float32,
            )
            if k:
                sums += sums_ref[half, span, columns]
            out_ref[half, span, :] = sums.astype(jnp.bfloat16)


def hidden_kernel(pos_ref, slot_ref, weight_ref, mine_ref, other_ref, out_ref, *, plan, at):
    for i, b, start, cap in plan.spans():
        block = pos_ref[at + b]
        chosen = picks(slot_ref, i, block, cap)
        scale = jnp.sum(jnp.where(chosen, weight_ref[i, pl.ds(block, 1), :], 0.0), axis=1, keepdims=True)
        span = slice(start, start + cap)
        gate = mine_ref[0, span, :].astype(jnp.float32) + other_ref[0, span, :].astype(jnp.float32)
        up = mine_ref[1, span, :].astype(jnp.float32) + other_ref[1, span, :].astype(jnp.float32)
        out_ref[span, :] = (gate / (1.0 + jnp.exp(-gate)) * up * scale).astype(jnp.bfloat16)


def down_kernel(first_ref, pos_ref, slot_ref, *refs, plan, at, part_at):
    pieces = refs[: plan.parts]
    down_ref, mine_ref, other_ref, dense_ref, tiles_ref, done = refs[plan.parts :]
    buffers, tile = tiles_ref.shape[0], tiles_ref.shape[3]
    copies = [
        pltpu.make_async_copy(
            down_ref.at[:, :, k * tile : (k + 1) * tile], tiles_ref.at[k % buffers], done.at[k]
        )
        for k in range(plan.feat // tile)
    ]
    for copy in copies[:buffers]:
        copy.start()
    first = first_ref[0]
    for i, b, start, cap in plan.spans():
        select = picks(slot_ref, i, pos_ref[at + b], cap).astype(jnp.bfloat16)
        for q, piece_ref in enumerate(pieces):
            offset = local_of(i, first) * plan.hidden + pos_ref[part_at + q] * plan.piece
            dense_ref[
                b * plan.tokens : (b + 1) * plan.tokens,
                pl.ds(pl.multiple_of(offset, LANES), plan.piece),
            ] = lax.dot_general(
                select,
                piece_ref[start : start + cap, :],
                (((0,), (0,)), ((), ())),
                preferred_element_type=jnp.float32,
            ).astype(jnp.bfloat16)

    for k, copy in enumerate(copies):
        copy.wait()
        weight = tiles_ref[k % buffers].reshape(plan.exp_dev * plan.hidden, tile)
        total = jnp.dot(dense_ref[...], weight, preferred_element_type=jnp.float32)
        span = slice(k * tile, (k + 1) * tile)
        mine_ref[:, span] = total[: plan.tokens].astype(jnp.bfloat16)
        other_ref[:, span] = total[plan.tokens :].astype(jnp.bfloat16)
        if k + buffers < len(copies):
            copies[k + buffers].start()


SMEM = pl.BlockSpec(memory_space=pltpu.SMEM)
VMEM = pl.BlockSpec(memory_space=pltpu.VMEM)
HBM = pl.BlockSpec(memory_space=pltpu.HBM)
PARAMS = pltpu.CompilerParams(vmem_limit_bytes=VMEM_LIMIT)
LONG = pl.CostEstimate(flops=30_000_000_000, bytes_accessed=1000, transcendentals=0)
COST = pl.CostEstimate(flops=1000, bytes_accessed=1000, transcendentals=0)


def after(x, *others):
    return lax.optimization_barrier((x, *others))[0]


class Order:
    def __init__(self, pos):
        self.pos = pos

    def follow(self, *results):
        self.pos = after(self.pos, *results)

    def run(self, call):
        result = call(self.pos)
        self.follow(*jax.tree.leaves(result))
        return result


def stored(x):
    return pltpu.with_memory_space_constraint(x, pltpu.HBM)


def call_route(plan, pos, infos):
    lists = jax.ShapeDtypeStruct((plan.exp_dev, plan.columns, plan.tokens), jnp.int32)
    return pl.pallas_call(
        functools.partial(route_kernel, plan=plan),
        out_shape=(
            lists,
            jax.ShapeDtypeStruct(lists.shape, jnp.float32),
            jax.ShapeDtypeStruct((1,), jnp.int32),
        ),
        in_specs=[SMEM] + [VMEM] * len(infos),
        out_specs=(VMEM, VMEM, SMEM),
        compiler_params=PARAMS,
        cost_estimate=COST,
        name="route",
    )(pos, *infos)


def call_up(plan, route, pos, mine, other, w_gate, w_up, at, part_at):
    slot, _, first = route
    pieces = 2 if plan.feat % (2 * LANES) == 0 else 1
    copies = 2 * plan.exp_dev * pieces
    out = jax.ShapeDtypeStruct((2, plan.rows, plan.piece), jnp.bfloat16)
    return pl.pallas_call(
        functools.partial(up_kernel, plan=plan, at=at, part_at=part_at),
        out_shape=(out,) * plan.parts,
        in_specs=[SMEM, SMEM] + [VMEM] * 3 + [HBM] * 2,
        out_specs=(VMEM,) * plan.parts,
        scratch_shapes=[
            pltpu.VMEM((plan.rows, plan.feat), jnp.bfloat16),
            pltpu.VMEM((2, plan.rows, plan.hidden), jnp.float32),
            pltpu.VMEM((copies, plan.feat // pieces, plan.hidden), jnp.bfloat16),
            pltpu.SemaphoreType.DMA((copies,)),
        ],
        compiler_params=pltpu.CompilerParams(vmem_limit_bytes=UP_LIMIT),
        cost_estimate=COST,
        name="gate_up",
    )(first, pos, slot, mine, other, stored(w_gate), stored(w_up))


def call_hidden(plan, route, pos, mine, other, at, cost):
    slot, weight, _ = route
    return pl.pallas_call(
        functools.partial(hidden_kernel, plan=plan, at=at),
        out_shape=jax.ShapeDtypeStruct((plan.rows, plan.piece), jnp.bfloat16),
        in_specs=[SMEM] + [VMEM] * 4,
        out_specs=VMEM,
        compiler_params=PARAMS,
        cost_estimate=cost,
        name="hidden",
    )(pos, slot, weight, mine, other)


def call_down(plan, route, pos, pieces, w_down, at, part_at, cost):
    slot, _, first = route
    tile = tile_of(plan.feat, 896)
    out = jax.ShapeDtypeStruct((plan.tokens, plan.feat), jnp.bfloat16)
    return pl.pallas_call(
        functools.partial(down_kernel, plan=plan, at=at, part_at=part_at),
        out_shape=(out, out),
        in_specs=[SMEM, SMEM] + [VMEM] * (1 + plan.parts) + [HBM],
        out_specs=(VMEM, VMEM),
        scratch_shapes=[
            pltpu.VMEM((CORES * plan.tokens, plan.exp_dev * plan.hidden), jnp.bfloat16),
            pltpu.VMEM((BUFFERS, plan.exp_dev, plan.hidden, tile), jnp.bfloat16),
            pltpu.SemaphoreType.DMA((plan.feat // tile,)),
        ],
        compiler_params=pltpu.CompilerParams(vmem_limit_bytes=DOWN_LIMIT),
        cost_estimate=cost,
        name="down",
    )(first, pos, slot, *pieces, stored(w_down))


def per_device(tokens, expert_ids, route_weights, w_gate, w_up, w_down):
    columns, parts = lax.axis_size("expert"), lax.axis_size("dp")
    chips = columns // CORES
    column, part = lax.axis_index("expert"), lax.axis_index("dp")
    chip, core = column // CORES, column % CORES
    plan = Plan(
        columns, w_gate.shape[0], *expert_ids.shape, tokens.shape[1], w_gate.shape[2], parts
    )

    def hop(x, pairs):
        return lax.ppermute(
            x, "expert", [(a * CORES + c, b * CORES + c) for a, b in pairs for c in range(CORES)]
        )

    def swap_cores(x):
        return lax.ppermute(x, "expert", [(i, i ^ 1) for i in range(columns)])

    values, at = [column], []

    def list_blocks(source):
        away = (chip - source) % chips
        at.append(len(values))
        values.extend([away, chips + away])

    if chips == 4:
        sources = [chip, chip ^ 1, chip ^ 2, 3 - chip]
    else:
        sources = [(chip - s) % chips for s in range(chips)]
    for source in sources:
        list_blocks(source)
    part_at = len(values)
    values += [part, 1 - part] if parts == 2 else list(range(parts))
    pos = jnp.stack([jnp.asarray(v, jnp.int32) for v in values])

    def shift(s):
        return [(z, (z + s) % chips) for z in range(chips)]

    info = jnp.concatenate([expert_ids.T.astype(jnp.float32), route_weights.T], axis=0)
    info = [info] + [hop(info, shift(s)) for s in range(1, chips)]
    sent = after(tokens, *info[1:])
    info = jnp.stack(info)
    infos = [info, swap_cores(info)]

    inner = (chip == 1) | (chip == 2)
    near, middle, outward = [(0, 1), (1, 0), (2, 3), (3, 2)], [(1, 2), (2, 1)], [(1, 0), (2, 3)]
    if chips == 4:
        first, third = hop(sent, near), hop(sent, middle)
    else:
        first, *rest = [hop(sent, shift(s)) for s in range(1, chips)] or [None]

    flip = [(0, 1), (1, 0)]
    order = Order(pos)
    route = order.run(lambda pos: call_route(plan, pos, infos))

    here, away, hidden, total, blocks = {}, {}, {}, {}, {}

    def begin(s):
        sums = order.run(
            lambda pos: call_up(plan, route, pos, *blocks[s], w_gate, w_up, at[s], part_at)
        )
        if parts == 2:
            here[s], away[s] = sums[0], lax.ppermute(sums[1], "dp", flip)
        else:
            both = jnp.stack(sums)
            here[s] = lax.psum_scatter(both, "dp", scatter_dimension=0)
            away[s] = jnp.zeros_like(here[s])

    def join(s):
        own = order.run(lambda pos: call_hidden(plan, route, pos, here[s], away[s], at[s], LONG if s else COST))
        if parts == 2:
            hidden[s] = [own, lax.ppermute(own, "dp", flip)]
        else:
            own = lax.all_gather(own, "dp", axis=0)
            hidden[s] = [own[q] for q in range(parts)]

    def down(s):
        kept, shared = order.run(
            lambda pos: call_down(plan, route, pos, hidden[s], w_down, at[s], part_at, LONG if s else COST)
        )
        total[s] = kept, swap_cores(shared)

    def send(s):
        summed = total[s][0].astype(jnp.float32) + total[s][1].astype(jnp.float32)
        relay = chips == 4 and s == 3
        if relay:
            (passed,) = total[2]
            summed += jnp.where(inner, passed, jnp.zeros_like(passed)).astype(jnp.float32)
            total[2] = (jnp.where(inner, jnp.zeros_like(passed), passed),)
        summed = summed.astype(jnp.bfloat16)
        order.follow(summed)
        if chips == 4:
            pairs = [near, [(0, 1), (1, 3), (2, 0), (3, 2)], [(0, 3), (1, 2), (2, 1), (3, 0)]][s - 1]
        else:
            pairs = shift(-s)
        total[s] = (hop(summed, pairs),)

    def take(s, block):
        blocks[s] = [block, swap_cores(block)]

    take(0, sent)
    begin(0)
    if chips == 4:
        first, third = after(first, order.pos), after(third, order.pos)
        take(1, first)
        relayed, other = hop(first, middle), hop(third, outward)
        begin(1)
        join(0)
        relayed = after(relayed, order.pos)
        take(2, jnp.where(inner, relayed, other))
        last = hop(relayed, outward)
        join(1)
        begin(2)
        down(1)
        take(3, jnp.where(inner, third, after(last, order.pos)))
        join(2)
        send(1)
        begin(3)
        down(2)
        join(3)
        order.follow(*total[1])
        send(2)
        down(3)
        send(3)
        order.follow(*total[2])
        down(0)
    else:
        join(0)
        down(0)
        for s in range(1, chips):
            take(s, [first, *rest][s - 1])
            begin(s)
            join(s)
            down(s)
            send(s)
    return sum(t.astype(jnp.float32) for s in range(chips) for t in total[s]).astype(jnp.bfloat16)


def solution(mesh):
    in_specs = (
        P(("group", "expert"), "dp"),
        P(("group", "expert"), None),
        P(("group", "expert"), None),
        P("expert", "dp", None),
        P("expert", "dp", None),
        P("expert", None, "dp"),
    )
    out_specs = P(("group", "expert"), "dp")
    return jax.shard_map(
        per_device, mesh=mesh, in_specs=in_specs, out_specs=out_specs, check_vma=False
    )
```

```python
import functools

import jax
import jax.numpy as jnp
from jax import lax
from jax.experimental import pallas as pl
from jax.experimental.pallas import tpu as pltpu
from jax.sharding import PartitionSpec as P

COPIES = 2
CORES = 2
LANES = 128
VMEM_LIMIT = 4 * 1024 * 1024
UP_LIMIT = 46 * 1024 * 1024
DOWN_LIMIT = 24 * 1024 * 1024
BUFFERS = 4


def capacities(token_column, selected_count, expert_table):
    slot_capacity = min(token_column * selected_count * 3 // (2 * expert_table), token_column // 2)
    popular_capacity = min(
        token_column, max(slot_capacity * 3 // 2, token_column * selected_count // expert_table)
    )
    return slot_capacity, popular_capacity


def round_up(value, unit):
    return -(-value // unit) * unit


def tile_of(size, most):
    return max(t for t in range(LANES, most + 1, LANES) if size % t == 0)


class Plan:
    def __init__(self, columns, exp_dev, token_column, selected_count, feat, hidden, parts):
        self.columns, self.exp_dev, self.tokens, self.topk = columns, exp_dev, token_column, selected_count
        self.feat, self.hidden, self.parts = feat, hidden, parts
        self.slot_cap, self.popular_cap = capacities(token_column, selected_count, columns * exp_dev)
        self.caps = [round_up(self.popular_cap, 16)] + [round_up(self.slot_cap, 16)] * (exp_dev - 1)
        self.starts = [CORES * sum(self.caps[:i]) for i in range(exp_dev)]
        self.rows = CORES * sum(self.caps)
        self.piece = hidden // parts

    def spans(self):
        for i, cap in enumerate(self.caps):
            for b in range(CORES):
                yield i, b, self.starts[i] + b * cap, cap


def local_of(i, first):
    return first if i == 0 else jnp.where(i - 1 < first, i - 1, i)


def route_kernel(pos_ref, *refs, plan):
    slot_ref, weight_ref, first_ref = refs[-3:]
    column = pos_ref[0]
    info = jnp.concatenate([ref[...] for ref in refs[:-3]], axis=0)
    ids = info[:, : plan.topk, :]
    weights = info[:, plan.topk :, :]
    totals = [
        jnp.sum((ids == float(e)).astype(jnp.float32)) for e in range(plan.columns * plan.exp_dev)
    ]
    loads, best = [], []
    for c in range(plan.columns):
        own = totals[c * plan.exp_dev : (c + 1) * plan.exp_dev]
        load, top, where = own[0], own[0], jnp.int32(0)
        for i in range(1, plan.exp_dev):
            load = load + own[i]
            where = jnp.where(own[i] > top, i, where)
            top = jnp.maximum(own[i], top)
        loads.append(load)
        best.append(where)
    heavy_here = jnp.int32(0)
    for _ in range(COPIES):
        top, where = loads[0], jnp.int32(0)
        for c in range(1, plan.columns):
            where = jnp.where(loads[c] > top, c, where)
            top = jnp.maximum(loads[c], top)
        heavy_here = jnp.where(where == column, 1, heavy_here)
        loads = [jnp.where(where == c, -1.0, loads[c]) for c in range(plan.columns)]
    own_best = jnp.int32(0)
    for c in range(plan.columns):
        own_best = jnp.where(column == c, best[c], own_best)
    first = jnp.where(heavy_here == 1, own_best, 0)
    first_ref[0] = first
    earlier = (
        lax.broadcasted_iota(jnp.int32, (plan.tokens, plan.tokens), 0)
        < lax.broadcasted_iota(jnp.int32, (plan.tokens, plan.tokens), 1)
    ).astype(jnp.bfloat16)
    for i in range(plan.exp_dev):
        expert = (column * plan.exp_dev + local_of(i, first)).astype(jnp.float32)
        hit = ids == expert
        named = jnp.sum(hit.astype(jnp.float32), axis=1)
        weight_ref[i] = jnp.sum(jnp.where(hit, weights, 0.0), axis=1)
        rank = jnp.dot(named.astype(jnp.bfloat16), earlier, preferred_element_type=jnp.float32)
        cap = jnp.int32(plan.slot_cap)
        if i == 0:
            cap = jnp.where(heavy_here == 1, plan.popular_cap, cap)
        rank = rank.astype(jnp.int32)
        slot_ref[i] = jnp.where((named > 0.5) & (rank < cap), rank, -1)


def picks(slot_ref, i, block, cap):
    row = slot_ref[i, pl.ds(block, 1), :]
    return lax.broadcasted_iota(jnp.int32, (cap, row.shape[1]), 0) == row


def up_kernel(
    first_ref, pos_ref, slot_ref, mine_ref, other_ref, gate_ref, up_ref, *refs, plan, at, part_at
):
    outs, (rows_ref, sums_ref, held_ref, done) = refs[: plan.parts], refs[plan.parts :]
    pieces = held_ref.shape[0] // (2 * plan.exp_dev)
    depth = held_ref.shape[1]
    first = first_ref[0]
    units = [(k, i, half) for k in range(pieces) for i in range(plan.exp_dev) for half in range(2)]
    copies = [
        pltpu.make_async_copy(
            (gate_ref, up_ref)[half].at[local_of(i, first), k * depth : (k + 1) * depth, :],
            held_ref.at[n],
            done.at[n],
        )
        for n, (k, i, half) in enumerate(units)
    ]
    for copy in copies:
        copy.start()
    step = tile_of(plan.feat, 512)
    for i, b, start, cap in plan.spans():
        select = picks(slot_ref, i, pos_ref[at + b], cap).astype(jnp.bfloat16)
        block_ref = (mine_ref, other_ref)[b]
        for k in range(0, plan.feat, step):
            rows_ref[start : start + cap, k : k + step] = jnp.dot(
                select, block_ref[:, k : k + step], preferred_element_type=jnp.float32
            ).astype(jnp.bfloat16)

    for n, (k, i, half) in enumerate(units):
        span = slice(plan.starts[i], plan.starts[i] + CORES * plan.caps[i])
        copies[n].wait()
        if k < pieces - 1:
            sums = jnp.dot(
                rows_ref[span, k * depth : (k + 1) * depth],
                held_ref[n],
                preferred_element_type=jnp.float32,
            )
            sums_ref[half, span, :] = sums if k == 0 else sums_ref[half, span, :] + sums
            continue
        for q, out_ref in enumerate(outs):
            columns = pl.ds(pl.multiple_of(pos_ref[part_at + q] * plan.piece, LANES), plan.piece)
            sums = jnp.dot(
                rows_ref[span, k * depth : (k + 1) * depth],
                held_ref[n, :, columns],
                preferred_element_type=jnp.float32,
            )
            if k:
                sums += sums_ref[half, span, columns]
            out_ref[half, span, :] = sums.astype(jnp.bfloat16)


def hidden_kernel(pos_ref, slot_ref, weight_ref, mine_ref, other_ref, out_ref, *, plan, at):
    for i, b, start, cap in plan.spans():
        block = pos_ref[at + b]
        chosen = picks(slot_ref, i, block, cap)
        scale = jnp.sum(jnp.where(chosen, weight_ref[i, pl.ds(block, 1), :], 0.0), axis=1, keepdims=True)
        span = slice(start, start + cap)
        gate = mine_ref[0, span, :].astype(jnp.float32) + other_ref[0, span, :].astype(jnp.float32)
        up = mine_ref[1, span, :].astype(jnp.float32) + other_ref[1, span, :].astype(jnp.float32)
        out_ref[span, :] = (gate / (1.0 + jnp.exp(-gate)) * up * scale).astype(jnp.bfloat16)


def down_kernel(first_ref, pos_ref, slot_ref, *refs, plan, at, part_at):
    pieces = refs[: plan.parts]
    down_ref, mine_ref, other_ref, dense_ref, tiles_ref, done = refs[plan.parts :]
    buffers, tile = tiles_ref.shape[0], tiles_ref.shape[3]
    copies = [
        pltpu.make_async_copy(
            down_ref.at[:, :, k * tile : (k + 1) * tile], tiles_ref.at[k % buffers], done.at[k]
        )
        for k in range(plan.feat // tile)
    ]
    for copy in copies[:buffers]:
        copy.start()
    first = first_ref[0]
    for i, b, start, cap in plan.spans():
        select = picks(slot_ref, i, pos_ref[at + b], cap).astype(jnp.bfloat16)
        for q, piece_ref in enumerate(pieces):
            offset = local_of(i, first) * plan.hidden + pos_ref[part_at + q] * plan.piece
            dense_ref[
                b * plan.tokens : (b + 1) * plan.tokens,
                pl.ds(pl.multiple_of(offset, LANES), plan.piece),
            ] = lax.dot_general(
                select,
                piece_ref[start : start + cap, :],
                (((0,), (0,)), ((), ())),
                preferred_element_type=jnp.float32,
            ).astype(jnp.bfloat16)

    for k, copy in enumerate(copies):
        copy.wait()
        weight = tiles_ref[k % buffers].reshape(plan.exp_dev * plan.hidden, tile)
        total = jnp.dot(dense_ref[...], weight, preferred_element_type=jnp.float32)
        span = slice(k * tile, (k + 1) * tile)
        mine_ref[:, span] = total[: plan.tokens].astype(jnp.bfloat16)
        other_ref[:, span] = total[plan.tokens :].astype(jnp.bfloat16)
        if k + buffers < len(copies):
            copies[k + buffers].start()


SMEM = pl.BlockSpec(memory_space=pltpu.SMEM)
VMEM = pl.BlockSpec(memory_space=pltpu.VMEM)
HBM = pl.BlockSpec(memory_space=pltpu.HBM)
PARAMS = pltpu.CompilerParams(vmem_limit_bytes=VMEM_LIMIT)
LONG = pl.CostEstimate(flops=30_000_000_000, bytes_accessed=1000, transcendentals=0)
COST = pl.CostEstimate(flops=1000, bytes_accessed=1000, transcendentals=0)


def after(x, *others):
    return lax.optimization_barrier((x, *others))[0] if others else x


class Order:
    def __init__(self, pos):
        self.pos = pos

    def follow(self, *results):
        self.pos = after(self.pos, *results)

    def run(self, call):
        result = call(self.pos)
        self.follow(*jax.tree.leaves(result))
        return result


def stored(x):
    return pltpu.with_memory_space_constraint(x, pltpu.HBM)


def call_route(plan, pos, infos):
    lists = jax.ShapeDtypeStruct((plan.exp_dev, plan.columns, plan.tokens), jnp.int32)
    return pl.pallas_call(
        functools.partial(route_kernel, plan=plan),
        out_shape=(
            lists,
            jax.ShapeDtypeStruct(lists.shape, jnp.float32),
            jax.ShapeDtypeStruct((1,), jnp.int32),
        ),
        in_specs=[SMEM] + [VMEM] * len(infos),
        out_specs=(VMEM, VMEM, SMEM),
        compiler_params=PARAMS,
        cost_estimate=COST,
        name="route",
    )(pos, *infos)


def call_up(plan, route, pos, mine, other, w_gate, w_up, at, part_at):
    slot, _, first = route
    pieces = 2 if plan.feat % (2 * LANES) == 0 else 1
    copies = 2 * plan.exp_dev * pieces
    out = jax.ShapeDtypeStruct((2, plan.rows, plan.piece), jnp.bfloat16)
    return pl.pallas_call(
        functools.partial(up_kernel, plan=plan, at=at, part_at=part_at),
        out_shape=(out,) * plan.parts,
        in_specs=[SMEM, SMEM] + [VMEM] * 3 + [HBM] * 2,
        out_specs=(VMEM,) * plan.parts,
        scratch_shapes=[
            pltpu.VMEM((plan.rows, plan.feat), jnp.bfloat16),
            pltpu.VMEM((2, plan.rows, plan.hidden), jnp.float32),
            pltpu.VMEM((copies, plan.feat // pieces, plan.hidden), jnp.bfloat16),
            pltpu.SemaphoreType.DMA((copies,)),
        ],
        compiler_params=pltpu.CompilerParams(vmem_limit_bytes=UP_LIMIT),
        cost_estimate=COST,
        name="gate_up",
    )(first, pos, slot, mine, other, stored(w_gate), stored(w_up))


def call_hidden(plan, route, pos, mine, other, at, cost):
    slot, weight, _ = route
    return pl.pallas_call(
        functools.partial(hidden_kernel, plan=plan, at=at),
        out_shape=jax.ShapeDtypeStruct((plan.rows, plan.piece), jnp.bfloat16),
        in_specs=[SMEM] + [VMEM] * 4,
        out_specs=VMEM,
        compiler_params=PARAMS,
        cost_estimate=cost,
        name="hidden",
    )(pos, slot, weight, mine, other)


def call_down(plan, route, pos, pieces, w_down, at, part_at, cost):
    slot, _, first = route
    tile = tile_of(plan.feat, 896)
    out = jax.ShapeDtypeStruct((plan.tokens, plan.feat), jnp.bfloat16)
    return pl.pallas_call(
        functools.partial(down_kernel, plan=plan, at=at, part_at=part_at),
        out_shape=(out, out),
        in_specs=[SMEM, SMEM] + [VMEM] * (1 + plan.parts) + [HBM],
        out_specs=(VMEM, VMEM),
        scratch_shapes=[
            pltpu.VMEM((CORES * plan.tokens, plan.exp_dev * plan.hidden), jnp.bfloat16),
            pltpu.VMEM((BUFFERS, plan.exp_dev, plan.hidden, tile), jnp.bfloat16),
            pltpu.SemaphoreType.DMA((plan.feat // tile,)),
        ],
        compiler_params=pltpu.CompilerParams(vmem_limit_bytes=DOWN_LIMIT),
        cost_estimate=cost,
        name="down",
    )(first, pos, slot, *pieces, stored(w_down))


def per_device(tokens, expert_ids, route_weights, w_gate, w_up, w_down):
    columns, parts = lax.axis_size("expert"), lax.axis_size("dp")
    chips = columns // CORES
    column, part = lax.axis_index("expert"), lax.axis_index("dp")
    chip, core = column // CORES, column % CORES
    plan = Plan(
        columns, w_gate.shape[0], *expert_ids.shape, tokens.shape[1], w_gate.shape[2], parts
    )

    def hop(x, pairs):
        return lax.ppermute(
            x, "expert", [(a * CORES + c, b * CORES + c) for a, b in pairs for c in range(CORES)]
        )

    def swap_cores(x):
        return lax.ppermute(x, "expert", [(i, i ^ 1) for i in range(columns)])

    values, at = [column], []

    def list_blocks(source):
        away = (chip - source) % chips
        at.append(len(values))
        values.extend([away, chips + away])

    if chips == 4:
        sources = [chip, chip ^ 1, chip ^ 2, 3 - chip]
    else:
        sources = [(chip - s) % chips for s in range(chips)]
    for source in sources:
        list_blocks(source)
    part_at = len(values)
    values += [part, 1 - part] if parts == 2 else list(range(parts))
    pos = jnp.stack([jnp.asarray(v, jnp.int32) for v in values])

    def shift(s):
        return [(z, (z + s) % chips) for z in range(chips)]

    info = jnp.concatenate([expert_ids.T.astype(jnp.float32), route_weights.T], axis=0)
    info = [info] + [hop(info, shift(s)) for s in range(1, chips)]
    sent = after(tokens, *info[1:])
    info = jnp.stack(info)
    infos = [info, swap_cores(info)]

    inner = (chip == 1) | (chip == 2)
    near, middle, outward = [(0, 1), (1, 0), (2, 3), (3, 2)], [(1, 2), (2, 1)], [(1, 0), (2, 3)]
    if chips == 4:
        first, third = hop(sent, near), hop(sent, middle)
    else:
        first, *rest = [hop(sent, shift(s)) for s in range(1, chips)] or [None]

    flip = [(0, 1), (1, 0)]
    order = Order(pos)
    route = order.run(lambda pos: call_route(plan, pos, infos))

    here, away, hidden, total, blocks = {}, {}, {}, {}, {}

    def begin(s):
        here[s], *away[s] = order.run(
            lambda pos: call_up(plan, route, pos, *blocks[s], w_gate, w_up, at[s], part_at)
        )

    def exchange(s, *others):
        if parts == 2:
            away[s] = lax.ppermute(after(*away[s], *others), "dp", flip)
        else:
            here[s] = lax.psum_scatter(jnp.stack([here[s], *away[s]]), "dp", scatter_dimension=0)
            away[s] = jnp.zeros_like(here[s])

    def join(s):
        own = order.run(lambda pos: call_hidden(plan, route, pos, here[s], away[s], at[s], LONG))
        if parts == 2:
            hidden[s] = [own, lax.ppermute(own, "dp", flip)]
        else:
            own = lax.all_gather(own, "dp", axis=0)
            hidden[s] = [own[q] for q in range(parts)]

    def down(s):
        kept, shared = order.run(
            lambda pos: call_down(plan, route, pos, hidden[s], w_down, at[s], part_at, COST if s != 2 else LONG)
        )
        total[s] = kept, swap_cores(shared)

    def send(s):
        summed = total[s][0].astype(jnp.float32) + total[s][1].astype(jnp.float32)
        relay = chips == 4 and s == 3
        if relay:
            (passed,) = total[2]
            summed += jnp.where(inner, passed, jnp.zeros_like(passed)).astype(jnp.float32)
            total[2] = (jnp.where(inner, jnp.zeros_like(passed), passed),)
        summed = summed.astype(jnp.bfloat16)
        order.follow(summed)
        if chips == 4:
            pairs = [near, [(0, 1), (1, 3), (2, 0), (3, 2)], [(0, 3), (1, 2), (2, 1), (3, 0)]][s - 1]
        else:
            pairs = shift(-s)
        total[s] = (hop(summed, pairs),)

    def take(s, block):
        blocks[s] = [block, swap_cores(block)]

    take(0, sent)
    if chips == 4:
        first, third = after(first, order.pos), after(third, order.pos)
        take(1, first)
        relayed, other = hop(first, middle), hop(third, outward)
        begin(1)
        exchange(1)
        begin(0)
        relayed = after(relayed, order.pos)
        take(2, jnp.where(inner, relayed, other))
        last = hop(relayed, outward)
        join(1)
        begin(2)
        exchange(2)
        down(1)
        take(3, jnp.where(inner, third, after(last, order.pos)))
        join(2)
        send(1)
        begin(3)
        exchange(3)
        down(2)
        join(3)
        order.follow(*total[1])
        send(2)
        exchange(0, hidden[3][-1])
        down(3)
        order.follow(*total[2])
        join(0)
        send(3)
        down(0)
    else:
        begin(0)
        exchange(0)
        join(0)
        down(0)
        for s in range(1, chips):
            take(s, [first, *rest][s - 1])
            begin(s)
            exchange(s)
            join(s)
            down(s)
            send(s)
    return sum(t.astype(jnp.float32) for s in range(chips) for t in total[s]).astype(jnp.bfloat16)


def solution(mesh):
    in_specs = (
        P(("group", "expert"), "dp"),
        P(("group", "expert"), None),
        P(("group", "expert"), None),
        P("expert", "dp", None),
        P("expert", "dp", None),
        P("expert", None, "dp"),
    )
    out_specs = P(("group", "expert"), "dp")
    return jax.shard_map(
        per_device, mesh=mesh, in_specs=in_specs, out_specs=out_specs, check_vma=False
    )
```

```python
import functools

import jax
import jax.numpy as jnp
from jax import lax
from jax.experimental import pallas as pl
from jax.experimental.pallas import tpu as pltpu
from jax.sharding import PartitionSpec as P

COPIES = 2
CORES = 2
LANES = 128
VMEM_LIMIT = 4 * 1024 * 1024
UP_LIMIT = 46 * 1024 * 1024
DOWN_LIMIT = 24 * 1024 * 1024
BUFFERS = 4


def capacities(token_column, selected_count, expert_table):
    slot_capacity = min(token_column * selected_count * 3 // (2 * expert_table), token_column // 2)
    popular_capacity = min(
        token_column, max(slot_capacity * 3 // 2, token_column * selected_count // expert_table)
    )
    return slot_capacity, popular_capacity


def round_up(value, unit):
    return -(-value // unit) * unit


def tile_of(size, most):
    return max(t for t in range(LANES, most + 1, LANES) if size % t == 0)


class Plan:
    def __init__(self, columns, exp_dev, token_column, selected_count, feat, hidden, parts):
        self.columns, self.exp_dev, self.tokens, self.topk = columns, exp_dev, token_column, selected_count
        self.feat, self.hidden, self.parts = feat, hidden, parts
        self.slot_cap, self.popular_cap = capacities(token_column, selected_count, columns * exp_dev)
        self.caps = [round_up(self.popular_cap, 16)] + [round_up(self.slot_cap, 16)] * (exp_dev - 1)
        self.starts = [CORES * sum(self.caps[:i]) for i in range(exp_dev)]
        self.rows = CORES * sum(self.caps)
        self.piece = hidden // parts

    def spans(self):
        for i, cap in enumerate(self.caps):
            for b in range(CORES):
                yield i, b, self.starts[i] + b * cap, cap


def local_of(i, first):
    return first if i == 0 else jnp.where(i - 1 < first, i - 1, i)


def route_kernel(pos_ref, *refs, plan):
    slot_ref, weight_ref, first_ref = refs[-3:]
    column = pos_ref[0]
    info = jnp.concatenate([ref[...] for ref in refs[:-3]], axis=0)
    ids = info[:, : plan.topk, :]
    weights = info[:, plan.topk :, :]
    totals = [
        jnp.sum((ids == float(e)).astype(jnp.float32)) for e in range(plan.columns * plan.exp_dev)
    ]
    loads, best = [], []
    for c in range(plan.columns):
        own = totals[c * plan.exp_dev : (c + 1) * plan.exp_dev]
        load, top, where = own[0], own[0], jnp.int32(0)
        for i in range(1, plan.exp_dev):
            load = load + own[i]
            where = jnp.where(own[i] > top, i, where)
            top = jnp.maximum(own[i], top)
        loads.append(load)
        best.append(where)
    heavy_here = jnp.int32(0)
    for _ in range(COPIES):
        top, where = loads[0], jnp.int32(0)
        for c in range(1, plan.columns):
            where = jnp.where(loads[c] > top, c, where)
            top = jnp.maximum(loads[c], top)
        heavy_here = jnp.where(where == column, 1, heavy_here)
        loads = [jnp.where(where == c, -1.0, loads[c]) for c in range(plan.columns)]
    own_best = jnp.int32(0)
    for c in range(plan.columns):
        own_best = jnp.where(column == c, best[c], own_best)
    first = jnp.where(heavy_here == 1, own_best, 0)
    first_ref[0] = first
    earlier = (
        lax.broadcasted_iota(jnp.int32, (plan.tokens, plan.tokens), 0)
        < lax.broadcasted_iota(jnp.int32, (plan.tokens, plan.tokens), 1)
    ).astype(jnp.bfloat16)
    for i in range(plan.exp_dev):
        expert = (column * plan.exp_dev + local_of(i, first)).astype(jnp.float32)
        hit = ids == expert
        named = jnp.sum(hit.astype(jnp.float32), axis=1)
        weight_ref[i] = jnp.sum(jnp.where(hit, weights, 0.0), axis=1)
        rank = jnp.dot(named.astype(jnp.bfloat16), earlier, preferred_element_type=jnp.float32)
        cap = jnp.int32(plan.slot_cap)
        if i == 0:
            cap = jnp.where(heavy_here == 1, plan.popular_cap, cap)
        rank = rank.astype(jnp.int32)
        slot_ref[i] = jnp.where((named > 0.5) & (rank < cap), rank, -1)


def picks(slot_ref, i, block, cap):
    row = slot_ref[i, pl.ds(block, 1), :]
    return lax.broadcasted_iota(jnp.int32, (cap, row.shape[1]), 0) == row


def up_kernel(
    first_ref, pos_ref, slot_ref, mine_ref, other_ref, gate_ref, up_ref, *refs, plan, at, part_at
):
    outs, (rows_ref, sums_ref, held_ref, done) = refs[: plan.parts], refs[plan.parts :]
    pieces = held_ref.shape[0] // (2 * plan.exp_dev)
    depth = held_ref.shape[1]
    first = first_ref[0]
    units = [(k, i, half) for k in range(pieces) for i in range(plan.exp_dev) for half in range(2)]
    copies = [
        pltpu.make_async_copy(
            (gate_ref, up_ref)[half].at[local_of(i, first), k * depth : (k + 1) * depth, :],
            held_ref.at[n],
            done.at[n],
        )
        for n, (k, i, half) in enumerate(units)
    ]
    for copy in copies:
        copy.start()
    step = tile_of(plan.feat, 512)
    for i, b, start, cap in plan.spans():
        select = picks(slot_ref, i, pos_ref[at + b], cap).astype(jnp.bfloat16)
        block_ref = (mine_ref, other_ref)[b]
        for k in range(0, plan.feat, step):
            rows_ref[start : start + cap, k : k + step] = jnp.dot(
                select, block_ref[:, k : k + step], preferred_element_type=jnp.float32
            ).astype(jnp.bfloat16)

    for n, (k, i, half) in enumerate(units):
        span = slice(plan.starts[i], plan.starts[i] + CORES * plan.caps[i])
        copies[n].wait()
        if k < pieces - 1:
            sums = jnp.dot(
                rows_ref[span, k * depth : (k + 1) * depth],
                held_ref[n],
                preferred_element_type=jnp.float32,
            )
            sums_ref[half, span, :] = sums if k == 0 else sums_ref[half, span, :] + sums
            continue
        for q, out_ref in enumerate(outs):
            columns = pl.ds(pl.multiple_of(pos_ref[part_at + q] * plan.piece, LANES), plan.piece)
            sums = jnp.dot(
                rows_ref[span, k * depth : (k + 1) * depth],
                held_ref[n, :, columns],
                preferred_element_type=jnp.float32,
            )
            if k:
                sums += sums_ref[half, span, columns]
            out_ref[half, span, :] = sums.astype(jnp.bfloat16)


def hidden_kernel(pos_ref, slot_ref, weight_ref, mine_ref, other_ref, out_ref, *, plan, at):
    for i, b, start, cap in plan.spans():
        block = pos_ref[at + b]
        chosen = picks(slot_ref, i, block, cap)
        scale = jnp.sum(jnp.where(chosen, weight_ref[i, pl.ds(block, 1), :], 0.0), axis=1, keepdims=True)
        span = slice(start, start + cap)
        gate = mine_ref[0, span, :].astype(jnp.float32) + other_ref[0, span, :].astype(jnp.float32)
        up = mine_ref[1, span, :].astype(jnp.float32) + other_ref[1, span, :].astype(jnp.float32)
        out_ref[span, :] = (gate / (1.0 + jnp.exp(-gate)) * up * scale).astype(jnp.bfloat16)


def down_kernel(first_ref, pos_ref, slot_ref, *refs, plan, at, part_at):
    pieces = refs[: plan.parts]
    down_ref, mine_ref, other_ref, dense_ref, tiles_ref, done = refs[plan.parts :]
    buffers, tile = tiles_ref.shape[0], tiles_ref.shape[3]
    copies = [
        pltpu.make_async_copy(
            down_ref.at[:, :, k * tile : (k + 1) * tile], tiles_ref.at[k % buffers], done.at[k]
        )
        for k in range(plan.feat // tile)
    ]
    for copy in copies[:buffers]:
        copy.start()
    first = first_ref[0]
    for i, b, start, cap in plan.spans():
        select = picks(slot_ref, i, pos_ref[at + b], cap).astype(jnp.bfloat16)
        for q, piece_ref in enumerate(pieces):
            offset = local_of(i, first) * plan.hidden + pos_ref[part_at + q] * plan.piece
            dense_ref[
                b * plan.tokens : (b + 1) * plan.tokens,
                pl.ds(pl.multiple_of(offset, LANES), plan.piece),
            ] = lax.dot_general(
                select,
                piece_ref[start : start + cap, :],
                (((0,), (0,)), ((), ())),
                preferred_element_type=jnp.float32,
            ).astype(jnp.bfloat16)

    for k, copy in enumerate(copies):
        copy.wait()
        weight = tiles_ref[k % buffers].reshape(plan.exp_dev * plan.hidden, tile)
        total = jnp.dot(dense_ref[...], weight, preferred_element_type=jnp.float32)
        span = slice(k * tile, (k + 1) * tile)
        mine_ref[:, span] = total[: plan.tokens].astype(jnp.bfloat16)
        other_ref[:, span] = total[plan.tokens :].astype(jnp.bfloat16)
        if k + buffers < len(copies):
            copies[k + buffers].start()


SMEM = pl.BlockSpec(memory_space=pltpu.SMEM)
VMEM = pl.BlockSpec(memory_space=pltpu.VMEM)
HBM = pl.BlockSpec(memory_space=pltpu.HBM)
PARAMS = pltpu.CompilerParams(vmem_limit_bytes=VMEM_LIMIT)
LONG = pl.CostEstimate(flops=30_000_000_000, bytes_accessed=1000, transcendentals=0)
COST = pl.CostEstimate(flops=1000, bytes_accessed=1000, transcendentals=0)


def after(x, *others):
    return lax.optimization_barrier((x, *others))[0] if others else x


class Order:
    def __init__(self, pos):
        self.pos = pos

    def follow(self, *results):
        self.pos = after(self.pos, *results)

    def run(self, call):
        result = call(self.pos)
        self.follow(*jax.tree.leaves(result))
        return result


def stored(x):
    return pltpu.with_memory_space_constraint(x, pltpu.HBM)


def call_route(plan, pos, infos):
    lists = jax.ShapeDtypeStruct((plan.exp_dev, plan.columns, plan.tokens), jnp.int32)
    return pl.pallas_call(
        functools.partial(route_kernel, plan=plan),
        out_shape=(
            lists,
            jax.ShapeDtypeStruct(lists.shape, jnp.float32),
            jax.ShapeDtypeStruct((1,), jnp.int32),
        ),
        in_specs=[SMEM] + [VMEM] * len(infos),
        out_specs=(VMEM, VMEM, SMEM),
        compiler_params=PARAMS,
        cost_estimate=COST,
        name="route",
    )(pos, *infos)


def call_up(plan, route, pos, mine, other, w_gate, w_up, at, part_at):
    slot, _, first = route
    pieces = 1
    copies = 2 * plan.exp_dev * pieces
    out = jax.ShapeDtypeStruct((2, plan.rows, plan.piece), jnp.bfloat16)
    return pl.pallas_call(
        functools.partial(up_kernel, plan=plan, at=at, part_at=part_at),
        out_shape=(out,) * plan.parts,
        in_specs=[SMEM, SMEM] + [VMEM] * 3 + [HBM] * 2,
        out_specs=(VMEM,) * plan.parts,
        scratch_shapes=[
            pltpu.VMEM((plan.rows, plan.feat), jnp.bfloat16),
            pltpu.VMEM((2, plan.rows, plan.hidden), jnp.float32),
            pltpu.VMEM((copies, plan.feat // pieces, plan.hidden), jnp.bfloat16),
            pltpu.SemaphoreType.DMA((copies,)),
        ],
        compiler_params=pltpu.CompilerParams(vmem_limit_bytes=UP_LIMIT),
        cost_estimate=COST,
        name="gate_up",
    )(first, pos, slot, mine, other, stored(w_gate), stored(w_up))


def call_hidden(plan, route, pos, mine, other, at, cost):
    slot, weight, _ = route
    return pl.pallas_call(
        functools.partial(hidden_kernel, plan=plan, at=at),
        out_shape=jax.ShapeDtypeStruct((plan.rows, plan.piece), jnp.bfloat16),
        in_specs=[SMEM] + [VMEM] * 4,
        out_specs=VMEM,
        compiler_params=PARAMS,
        cost_estimate=cost,
        name="hidden",
    )(pos, slot, weight, mine, other)


def call_down(plan, route, pos, pieces, w_down, at, part_at, cost):
    slot, _, first = route
    tile = tile_of(plan.feat, 896)
    out = jax.ShapeDtypeStruct((plan.tokens, plan.feat), jnp.bfloat16)
    return pl.pallas_call(
        functools.partial(down_kernel, plan=plan, at=at, part_at=part_at),
        out_shape=(out, out),
        in_specs=[SMEM, SMEM] + [VMEM] * (1 + plan.parts) + [HBM],
        out_specs=(VMEM, VMEM),
        scratch_shapes=[
            pltpu.VMEM((CORES * plan.tokens, plan.exp_dev * plan.hidden), jnp.bfloat16),
            pltpu.VMEM((BUFFERS, plan.exp_dev, plan.hidden, tile), jnp.bfloat16),
            pltpu.SemaphoreType.DMA((plan.feat // tile,)),
        ],
        compiler_params=pltpu.CompilerParams(vmem_limit_bytes=DOWN_LIMIT),
        cost_estimate=cost,
        name="down",
    )(first, pos, slot, *pieces, stored(w_down))


def per_device(tokens, expert_ids, route_weights, w_gate, w_up, w_down):
    columns, parts = lax.axis_size("expert"), lax.axis_size("dp")
    chips = columns // CORES
    column, part = lax.axis_index("expert"), lax.axis_index("dp")
    chip, core = column // CORES, column % CORES
    plan = Plan(
        columns, w_gate.shape[0], *expert_ids.shape, tokens.shape[1], w_gate.shape[2], parts
    )

    def hop(x, pairs):
        return lax.ppermute(
            x, "expert", [(a * CORES + c, b * CORES + c) for a, b in pairs for c in range(CORES)]
        )

    def swap_cores(x):
        return lax.ppermute(x, "expert", [(i, i ^ 1) for i in range(columns)])

    values, at = [column], []

    def list_blocks(source):
        away = (chip - source) % chips
        at.append(len(values))
        values.extend([away, chips + away])

    if chips == 4:
        sources = [chip, chip ^ 1, chip ^ 2, 3 - chip]
    else:
        sources = [(chip - s) % chips for s in range(chips)]
    for source in sources:
        list_blocks(source)
    part_at = len(values)
    values += [part, 1 - part] if parts == 2 else list(range(parts))
    pos = jnp.stack([jnp.asarray(v, jnp.int32) for v in values])

    def shift(s):
        return [(z, (z + s) % chips) for z in range(chips)]

    info = jnp.concatenate([expert_ids.T.astype(jnp.float32), route_weights.T], axis=0)
    info = [info] + [hop(info, shift(s)) for s in range(1, chips)]
    sent = after(tokens, *info[1:])
    info = jnp.stack(info)
    infos = [info, swap_cores(info)]

    inner = (chip == 1) | (chip == 2)
    near, middle, outward = [(0, 1), (1, 0), (2, 3), (3, 2)], [(1, 2), (2, 1)], [(1, 0), (2, 3)]
    if chips == 4:
        first, third = hop(sent, near), hop(sent, middle)
    else:
        first, *rest = [hop(sent, shift(s)) for s in range(1, chips)] or [None]

    flip = [(0, 1), (1, 0)]
    order = Order(pos)
    route = order.run(lambda pos: call_route(plan, pos, infos))

    here, away, hidden, total, blocks = {}, {}, {}, {}, {}

    def begin(s):
        here[s], *away[s] = order.run(
            lambda pos: call_up(plan, route, pos, *blocks[s], w_gate, w_up, at[s], part_at)
        )

    def exchange(s, *others):
        if parts == 2:
            away[s] = lax.ppermute(after(*away[s], *others), "dp", flip)
        else:
            here[s] = lax.psum_scatter(jnp.stack([here[s], *away[s]]), "dp", scatter_dimension=0)
            away[s] = jnp.zeros_like(here[s])

    def join(s):
        own = order.run(lambda pos: call_hidden(plan, route, pos, here[s], away[s], at[s], LONG))
        if parts == 2:
            hidden[s] = [own, lax.ppermute(own, "dp", flip)]
        else:
            own = lax.all_gather(own, "dp", axis=0)
            hidden[s] = [own[q] for q in range(parts)]

    def down(s):
        kept, shared = order.run(
            lambda pos: call_down(plan, route, pos, hidden[s], w_down, at[s], part_at, COST if s != 2 else LONG)
        )
        total[s] = kept, swap_cores(shared)

    def send(s):
        summed = total[s][0].astype(jnp.float32) + total[s][1].astype(jnp.float32)
        relay = chips == 4 and s == 3
        if relay:
            (passed,) = total[2]
            summed += jnp.where(inner, passed, jnp.zeros_like(passed)).astype(jnp.float32)
            total[2] = (jnp.where(inner, jnp.zeros_like(passed), passed),)
        summed = summed.astype(jnp.bfloat16)
        order.follow(summed)
        if chips == 4:
            pairs = [near, [(0, 1), (1, 3), (2, 0), (3, 2)], [(0, 3), (1, 2), (2, 1), (3, 0)]][s - 1]
        else:
            pairs = shift(-s)
        total[s] = (hop(summed, pairs),)

    def take(s, block):
        blocks[s] = [block, swap_cores(block)]

    take(0, sent)
    if chips == 4:
        first, third = after(first, order.pos), after(third, order.pos)
        take(1, first)
        relayed, other = hop(first, middle), hop(third, outward)
        begin(1)
        exchange(1)
        begin(0)
        relayed = after(relayed, order.pos)
        take(2, jnp.where(inner, relayed, other))
        last = hop(relayed, outward)
        join(1)
        begin(2)
        exchange(2)
        down(1)
        take(3, jnp.where(inner, third, after(last, order.pos)))
        join(2)
        send(1)
        begin(3)
        exchange(3)
        down(2)
        join(3)
        order.follow(*total[1])
        send(2)
        exchange(0, hidden[3][-1])
        down(3)
        order.follow(*total[2])
        join(0)
        send(3)
        down(0)
    else:
        begin(0)
        exchange(0)
        join(0)
        down(0)
        for s in range(1, chips):
            take(s, [first, *rest][s - 1])
            begin(s)
            exchange(s)
            join(s)
            down(s)
            send(s)
    return sum(t.astype(jnp.float32) for s in range(chips) for t in total[s]).astype(jnp.bfloat16)


def solution(mesh):
    in_specs = (
        P(("group", "expert"), "dp"),
        P(("group", "expert"), None),
        P(("group", "expert"), None),
        P("expert", "dp", None),
        P("expert", "dp", None),
        P("expert", None, "dp"),
    )
    out_specs = P(("group", "expert"), "dp")
    return jax.shard_map(
        per_device, mesh=mesh, in_specs=in_specs, out_specs=out_specs, check_vma=False
    )
```
